1024 devices in a mesh: dp: 128 (over y, x, core), fsdp: 8 (over z).
Axes of the slice: x: 8, y: 8, z: 8, core: 2. Of those that a mesh axis runs over, the one named last changes fastest.
Arguments:
- tokens: bfloat16 [65536, 8192], P('dp', 'fsdp'), may hold values from -6 to 6
- frozen_value_weight: bfloat16 [8192, 512], P('fsdp'), may hold values from -0.0625 to 0.0625
- down_factor_rows: bfloat16 [512, 8192], P(None, 'fsdp'), may hold values from -6 to 6
- up_factor_rows: bfloat16 [512, 512], P(None, 'fsdp'), may hold values from -6 to 6
- cotangent: bfloat16 [65536, 512], P('dp', 'fsdp'), may hold values from -6 to 6
- row_adapter_index: int32 [65536, 1], P('dp'), may hold values from 0 to 31
- down_master_copy: float32 [512, 8192], P('dp', 'fsdp'), may hold values from -0.4375 to 0.4375
- up_master_copy: float32 [512, 512], P('dp', 'fsdp'), may hold values from -0.4375 to 0.4375
- down_first_moment: float32 [512, 8192], P('dp', 'fsdp'), may hold values from -0.005859375 to 0.005859375
- down_second_moment: float32 [512, 8192], P('dp', 'fsdp'), may hold values from 5.722046e-09 to 5.7220458e-08
- up_first_moment: float32 [512, 512], P('dp', 'fsdp'), may hold values from -0.0234375 to 0.0234375
- up_second_moment: float32 [512, 512], P('dp', 'fsdp'), may hold values from 9.1552735e-08 to 9.155273e-07
Outputs:
- mixed: bfloat16 [65536, 512], P('dp', 'fsdp')
- new_master_a: float32 [512, 8192], P('dp', 'fsdp')
- new_master_b: float32 [512, 512], P('dp', 'fsdp')
- new_first_a: float32 [512, 8192], P('dp', 'fsdp')
- new_second_a: float32 [512, 8192], P('dp', 'fsdp')
- new_first_b: float32 [512, 512], P('dp', 'fsdp')
- new_second_b: float32 [512, 512], P('dp', 'fsdp')
- returned_a: bfloat16 [512, 8192], P(None, 'fsdp')
- returned_b: bfloat16 [512, 512], P(None, 'fsdp')
The draws below stay inside these ranges and needn't reach their ends.
Inputs may be any that keep to these rules, and one draw needn't show every extreme that they name: `row_adapter_index`: every adapter names some row.
All inputs are finite; a program needn't handle non-finite values.
Results may differ from the reference program's by a relative error of at most 0.0042.
Values may be sent and summed in bfloat16 or wider, within the bound.
A program may use at most 32 MiB of HBM per device.

```python
import math
import jax
import jax.numpy as jnp
from jax import lax

MODEL_WIDTH = 8192
KEY_VALUE_WIDTH = 512
RANK = 16
LOCAL_ADAPTERS = 32
STEP = 10
PACKED_TOKENS = 65536
FACTOR_ROWS = 512


def level_of(key, dims, shards, least, largest):
    factor_of, own = 1.0, jax.random.fold_in(key, 6)
    for position, parts in shards:
        heights = jnp.exp(jax.random.uniform(jax.random.fold_in(own, position), (parts,), jnp.float32, least / len(shards), largest / len(shards)))
        factor_of = factor_of * jnp.repeat(heights, dims[position] // parts).reshape([-1 if axis == position else 1 for axis in range(len(dims))])
    return factor_of


def choose_distinct(stream_key, rows, count, top, lift):
    order = jax.random.permutation(jax.random.fold_in(stream_key, 1), count)
    favour = order
    for power in range(3):
        favour = favour * favour // count
    favour = favour * lift // count
    chance = jax.random.randint(jax.random.fold_in(stream_key, 2), (rows, count), 0, 4096) + favour
    fixed_rows = jax.random.permutation(jax.random.fold_in(stream_key, 3), rows)[jnp.arange(count) % rows]
    chance = jnp.where(jnp.arange(rows)[:, None] == fixed_rows[None, :], 1 << 14, chance)
    score = chance * count + jnp.arange(count)
    return lax.top_k(score.astype(jnp.int32), top)[1].astype(jnp.int32)


def centred(own_key, dims, deviation, limit, split=(), held_as=jnp.bfloat16):
    drawn = jax.random.normal(own_key, dims, jnp.float32) * deviation
    if len(split) > 0:
        drawn = level_of(own_key, dims, split, -0.22, 0.18) * drawn
    return jnp.clip(drawn, min=-limit, max=limit).astype(held_as)


def setup_inputs(seed: int = 0) -> dict:
    arg_keys = jax.random.split(jax.random.key(seed), 13)
    tokens = centred(arg_keys[0], (PACKED_TOKENS, MODEL_WIDTH), 1.0, 6.0, ((0, 128), (1, 8)))
    frozen_value_weight = centred(arg_keys[1], (MODEL_WIDTH, KEY_VALUE_WIDTH), MODEL_WIDTH ** -0.5, 0.0625, ((0, 8),))
    down_factor_rows = centred(arg_keys[2], (FACTOR_ROWS, MODEL_WIDTH), 1.0, 6.0, ((1, 8),))
    up_factor_rows = centred(arg_keys[3], (FACTOR_ROWS, KEY_VALUE_WIDTH), 1.0, 6.0, ((1, 8),))
    cotangent = centred(arg_keys[4], (PACKED_TOKENS, KEY_VALUE_WIDTH), 1.0, 6.0, ((0, 128), (1, 8)))
    row_adapter_index = choose_distinct(arg_keys[5], PACKED_TOKENS, LOCAL_ADAPTERS, 1, 512)
    down_master_copy = centred(arg_keys[6], (FACTOR_ROWS, MODEL_WIDTH), 0.03, 0.4375, ((0, 128), (1, 8)), jnp.float32)
    up_master_copy = centred(arg_keys[7], (FACTOR_ROWS, KEY_VALUE_WIDTH), 0.03, 0.4375, ((0, 128), (1, 8)), jnp.float32)
    down_first_moment = centred(arg_keys[8], (FACTOR_ROWS, MODEL_WIDTH), (0.075 * (KEY_VALUE_WIDTH * LOCAL_ADAPTERS / (MODEL_WIDTH * PACKED_TOKENS)) ** 0.5), 0.005859375, ((0, 128), (1, 8)), jnp.float32)
    down_second_moment = jnp.clip(jnp.exp(math.log(5.7220457705398076e-08) - 2.3025851 * jax.random.uniform(arg_keys[9], (FACTOR_ROWS, MODEL_WIDTH), jnp.float32) ** level_of(arg_keys[9], (FACTOR_ROWS, MODEL_WIDTH), ((0, 128), (1, 8)), -0.2, 0.2)), 5.7220459481754915e-09, 5.7220457705398076e-08)
    up_first_moment = centred(arg_keys[10], (FACTOR_ROWS, KEY_VALUE_WIDTH), (0.075 * (LOCAL_ADAPTERS / PACKED_TOKENS) ** 0.5), 0.0234375, ((0, 128), (1, 8)), jnp.float32)
    up_second_moment = jnp.clip(jnp.exp(math.log(9.155273232863692e-07) - 2.3025851 * jax.random.uniform(arg_keys[11], (FACTOR_ROWS, KEY_VALUE_WIDTH), jnp.float32) ** level_of(arg_keys[11], (FACTOR_ROWS, KEY_VALUE_WIDTH), ((0, 128), (1, 8)), -0.2, 0.2)), 9.155273517080786e-08, 9.155273232863692e-07)
    return dict(tokens=tokens, frozen_value_weight=frozen_value_weight, down_factor_rows=down_factor_rows, up_factor_rows=up_factor_rows, cotangent=cotangent, row_adapter_index=row_adapter_index, down_master_copy=down_master_copy, up_master_copy=up_master_copy, down_first_moment=down_first_moment, down_second_moment=down_second_moment, up_first_moment=up_first_moment, up_second_moment=up_second_moment)


BETA_ONE = 0.9
BETA_TWO = 0.999
ADAM_EPS = 1e-08
LEARN_RATE = 0.01

def select_ranks(values, member):
    total = values.shape[0]
    return lax.optimization_barrier(jnp.sum((values * member).reshape(total, LOCAL_ADAPTERS, RANK), axis=1))

def adam_step(master, moment_one, moment_two, gradient):
    new_one = BETA_ONE * moment_one + (1.0 - BETA_ONE) * gradient
    new_two = BETA_TWO * moment_two + (1.0 - BETA_TWO) * gradient * gradient
    fix_one = 1.0 - BETA_ONE ** STEP
    fix_two = 1.0 - BETA_TWO ** STEP
    update = new_one / fix_one / (jnp.sqrt(new_two / fix_two) + ADAM_EPS)
    return (master - LEARN_RATE * update, new_one, new_two)

def reference(tokens, frozen_value_weight, down_factor_rows, up_factor_rows, cotangent, row_adapter_index, down_master_copy, up_master_copy, down_first_moment, down_second_moment, up_first_moment, up_second_moment):
    input_scale = 1.0 / MODEL_WIDTH ** 0.5
    adapter_of = row_adapter_index[:, 0]
    onehot = (adapter_of[:, None] == jnp.arange(LOCAL_ADAPTERS, dtype=jnp.int32)[None, :]).astype(jnp.float32)
    member = jnp.repeat(onehot, RANK, axis=1)
    base_output = jnp.dot(tokens, frozen_value_weight, preferred_element_type=jnp.float32)
    projected_rows = jnp.dot(tokens, down_factor_rows.T, preferred_element_type=jnp.float32) * input_scale
    ranks = select_ranks(projected_rows, member).astype(jnp.bfloat16)
    spread_rows = (jnp.tile(ranks.astype(jnp.float32), (1, LOCAL_ADAPTERS)) * member).astype(jnp.bfloat16)
    mixed = (base_output + 0.25 * jnp.dot(spread_rows, up_factor_rows, preferred_element_type=jnp.float32)).astype(jnp.bfloat16)
    backward_pass = jnp.dot(cotangent, up_factor_rows.T, preferred_element_type=jnp.float32)
    rank_grads = (0.25 * select_ranks(backward_pass, member)).astype(jnp.bfloat16)
    grad_spread = (jnp.tile(rank_grads.astype(jnp.float32), (1, LOCAL_ADAPTERS)) * member).astype(jnp.bfloat16)
    counts = lax.optimization_barrier(jnp.sum(member, axis=0))
    grad_a = jnp.dot(grad_spread.T, tokens, preferred_element_type=jnp.float32) * input_scale / counts[:, None]
    grad_b = 0.25 * jnp.dot(spread_rows.T, cotangent, preferred_element_type=jnp.float32) / counts[:, None]
    new_master_a, new_first_a, new_second_a = adam_step(down_master_copy, down_first_moment, down_second_moment, grad_a)
    new_master_b, new_first_b, new_second_b = adam_step(up_master_copy, up_first_moment, up_second_moment, grad_b)
    return (mixed, new_master_a, new_master_b, new_first_a, new_second_a, new_first_b, new_second_b, new_master_a.astype(jnp.bfloat16), new_master_b.astype(jnp.bfloat16))
```

```python
import functools

import jax
import jax.numpy as jnp
from jax import lax
from jax.experimental import pallas as pl
from jax.experimental.pallas import tpu as pltpu
from jax.sharding import PartitionSpec as P

YS, XS, ZS = 8, 8, 8
MODEL_WIDTH = 8192
RANK = 16
STEP = 10
BETA_ONE = 0.9
BETA_TWO = 0.999
ADAM_EPS = 1e-08
LEARN_RATE = 0.01
SCALE = 1.0 / MODEL_WIDTH**0.5

MESH = pl.DeviceIdType.MESH
F32 = jnp.float32
BF16 = jnp.bfloat16
T = 512
D = 1024
Q = 64
LANES = 128


def adam_step(master, moment_one, moment_two, gradient):
    new_one = BETA_ONE * moment_one + (1.0 - BETA_ONE) * gradient
    new_two = BETA_TWO * moment_two + (1.0 - BETA_TWO) * gradient * gradient
    fix_one = 1.0 - BETA_ONE**STEP
    fix_two = 1.0 - BETA_TWO**STEP
    update = new_one / fix_one / (jnp.sqrt(new_two / fix_two) + ADAM_EPS)
    return (master - LEARN_RATE * update, new_one, new_two)


def far_first(n):
    return sorted(range(1, n), key=lambda k: -min(k, n - k))


def scratch(ys, xs, zs):
    ms = xs // 2
    nb = ms // 2
    c = ys * ms * RANK
    bz = 8 // zs
    v = pltpu.VMEM
    dma = pltpu.SemaphoreType.DMA
    bufs = dict(
        tok=v((T, D), BF16),
        down=v((c, D), BF16),
        w=v((D, zs * Q), BF16),
        proj=v((c, T), F32),
        spread_r=v((c, T), BF16),
        spread_g=v((c, T), BF16),
        gx=v((zs, bz * 8, LANES), F32),
        gr=v((zs, bz * 8, LANES), F32),
        gg=v((zs, bz * 8, LANES), F32),
        rx=v((zs, bz * 8, LANES), F32),
        rr=v((zs, bz * 8, LANES), F32),
        rg=v((zs, bz * 8, LANES), F32),
        bx=v((zs, T // 2, LANES), BF16),
        br=v((zs, T // 2, LANES), BF16),
        c0=v((8, LANES), F32),
        c0r=v((8, LANES), F32),
        c1=v((8, LANES), F32),
        c1r=v((xs, 8, LANES), F32),
        c2=v((8, LANES), F32),
        c2r=v((ys, 8, LANES), F32),
        pfx=v((4, 3, 4, 256), F32),
        pfr=v((4, 3, 4, 256), F32),
        sx=v((2, c, 256), F32),
        sr=v((2, c, 256), F32),
        own=v((2, c, 256), F32),
        sbx=v((ys, nb, RANK, LANES), F32),
        sbr=v((ys, nb, RANK, LANES), F32),
        a1x=v((xs, ys, RANK, LANES), BF16),
        a1r=v((xs, ys, RANK, LANES), BF16),
        a2x=v((ys, RANK, LANES), F32),
        a2r=v((ys, RANK, LANES), F32),
        b1x=v((ys, xs + nb, RANK, LANES), BF16),
        b1r=v((ys, xs + nb, RANK, LANES), BF16),
        b2x=v((xs, 2, RANK, LANES), F32),
        b2r=v((xs, 2, RANK, LANES), F32),
        g4=v((4, 4, 256), F32),
        g4r=v((4, 4, 256), F32),
        bq=v((4, 4, Q), F32),
        tile_b=v((RANK, LANES), BF16),
        rows=v((ys, ms, RANK, D), BF16),
        bg=v((xs, RANK, LANES), BF16),
        bt=v((ys, nb, RANK, LANES), BF16),
        bs=v((ys, nb, RANK, LANES), BF16),
        ball=v((c, LANES), F32),
    )
    sems = dict(
        load=3, gz1=zs, gz2=zs, rz1=zs, rz2=zs, bz=zs, cc=1, cx=xs, cy=ys, pf=4, sib=3,
        a1=xs, b1=ys, a2=ys, b2=xs, ret=4, ay=ys, ax=xs, bx_=xs, by=ys, bbx=xs, bby=ys, bbs=1,
        fa=xs, fb=ys, out=1,
    )
    local = ("load", "out")
    order = list(bufs)
    shapes = list(bufs.values())
    for name, n in sems.items():
        order.append(name + "_s")
        shapes.append(dma((n,)))
        if name not in local:
            order.append(name + "_r")
            shapes.append(dma((n,)))
    return order, shapes


INPUTS = ("tok_h", "w_h", "down_h", "up", "cot", "idx", "ma", "mb", "fa_", "sa", "fb_", "sb")
OUTPUTS = ("mixed", "nma", "nmb", "nfa", "nsa", "nfb", "nsb", "reta", "retb")


class Refs:
    def __init__(self, names, refs):
        self.__dict__.update(zip(names, refs))


def kernel(ys, xs, zs, order, *refs):
    r = Refs(INPUTS + OUTPUTS + tuple(order), refs)
    ms = xs // 2
    nb = ms // 2
    na = ys * ms
    c_rows = na * RANK
    bz = 8 // zs
    dp, z = lax.axis_index("dp"), lax.axis_index("fsdp")
    core = dp % 2
    x = (dp // 2) % xs
    y = dp // (2 * xs)
    h, m = x % 2, x // 2
    q = 2 * h + core
    half = core * (D // 2)
    other_half = (1 - core) * (D // 2)

    def at(yy=None, xx=None, cc=None, zz=None):
        yy = y if yy is None else yy
        xx = x if xx is None else xx
        cc = core if cc is None else cc
        return ((yy * xs + xx) * 2 + cc, z if zz is None else zz)

    started = []

    def send(src, dst, name, slot, device):
        copy = pltpu.make_async_remote_copy(
            src_ref=src,
            dst_ref=dst,
            send_sem=getattr(r, name + "_s").at[slot],
            recv_sem=getattr(r, name + "_r").at[slot],
            device_id=device,
            device_id_type=MESH,
        )
        copy.start()
        started.append(copy)
        return copy

    def xp(k):
        return lax.rem(x + k, xs)

    def yp(k):
        return lax.rem(y + k, ys)

    def zp(k):
        return lax.rem(z + k, zs)

    def from_x(k):
        return lax.rem(x + xs - k, xs)

    def from_y(k):
        return lax.rem(y + ys - k, ys)

    sibling = at(cc=1 - core)
    kx, ky, kz = far_first(xs), far_first(ys), far_first(zs)

    load_tok = pltpu.make_async_copy(r.tok_h, r.tok, r.load_s.at[0])
    load_down = pltpu.make_async_copy(r.down_h, r.down, r.load_s.at[1])
    load_w = pltpu.make_async_copy(r.w_h, r.w, r.load_s.at[2])
    load_down.start()
    load_tok.start()
    load_w.start()

    barrier = pltpu.get_barrier_semaphore()
    partners = [at(zz=zp(k)) for k in kz] + [at(xx=xp(k)) for k in kx] + [at(yy=yp(k)) for k in ky]
    x_pair = x + 1 - 2 * h
    partners += [sibling, at(xx=x_pair, cc=1 - core)]
    for device in partners:
        pl.semaphore_signal(barrier, inc=1, device_id=device, device_id_type=MESH)

    idx = r.idx[...]
    idx16 = jnp.broadcast_to(idx, (RANK, T))

    def chosen(values):
        total = jnp.zeros((RANK, T), F32)
        for a in range(na):
            total = jnp.where(idx16 == a, values[a * RANK : (a + 1) * RANK, :], total)
        return total

    def to_blocks(values, ref):
        for b in range(8):
            kh, tb = b // 4, b % 4
            ref[b // bz, (b % bz) * 8 : (b % bz) * 8 + 8, :] = values[
                kh * 8 : kh * 8 + 8, tb * LANES : (tb + 1) * LANES
            ]

    def from_blocks(ref):
        halves = []
        for kh in range(2):
            parts = []
            for tb in range(4):
                b = kh * 4 + tb
                parts.append(ref[b // bz, (b % bz) * 8 : (b % bz) * 8 + 8, :])
            halves.append(jnp.concatenate(parts, axis=1))
        return jnp.concatenate(halves, axis=0)

    def spread_into(values, ref):
        for a in range(na):
            ref[a * RANK : (a + 1) * RANK, :] = jnp.where(idx16 == a, values, 0.0).astype(BF16)

    r.proj[...] = lax.dot_general(
        r.up[...], r.cot[...], (((0,), (0,)), ((), ())), preferred_element_type=F32
    )
    to_blocks(chosen(r.proj), r.gx)
    ids = lax.broadcasted_iota(jnp.int32, (LANES, T), 0)
    onehot = jnp.where(ids == jnp.broadcast_to(idx, (LANES, T)), 1.0, 0.0).astype(BF16)
    counts = lax.dot_general(
        jnp.ones((8, T), BF16), onehot, (((1,), (1,)), ((), ())), preferred_element_type=F32
    )
    r.c0[...] = counts
    for j in range(4):
        hj, cj = j // 2, j % 2
        for i, ref in enumerate((r.ma, r.fa_, r.sa)):
            col = cj * (D // 2) + hj * LANES
            r.pfx[j, i, :, 0:LANES] = ref[:, col : col + LANES]
            r.pfx[j, i, :, LANES : 2 * LANES] = ref[:, col + 256 : col + 256 + LANES]

    pl.semaphore_wait(barrier, len(partners))

    gz1 = [(k, send(r.gx.at[zp(k)], r.gr.at[k], "gz1", k, at(zz=zp(k)))) for k in kz]
    cc = send(r.c0, r.c0r, "cc", 0, sibling)
    pf = []
    for k in range(1, 4):
        hk, ck = k // 2, k % 2
        h2 = h + hk - 2 * h * hk
        c2 = core + ck - 2 * core * ck
        pf.append(
            send(
                r.pfx.at[2 * h2 + c2], r.pfr.at[q], "pf", k, at(xx=2 * m + h2, cc=c2)
            )
        )

    load_down.wait()
    load_tok.wait()
    r.proj[...] = lax.dot_general(
        r.down[...], r.tok[...], (((1,), (1,)), ((), ())), preferred_element_type=F32
    )
    to_blocks(chosen(r.proj), r.rx)
    rz1 = [(k, send(r.rx.at[zp(k)], r.rr.at[k], "rz1", k, at(zz=zp(k)))) for k in kz]

    total = r.gx[z]
    for k, copy in gz1:
        copy.wait_recv()
        total = total + r.gr[k]
    r.gg[z] = (0.25 * total).astype(BF16).astype(F32)
    gz2 = [(k, send(r.gg.at[z], r.gg.at[z], "gz2", k, at(zz=zp(k)))) for k in kz]

    load_w.wait()
    lane = lax.broadcasted_iota(jnp.int32, (T // 2, LANES), 1)
    for i in range(zs // 2):
        part = jnp.dot(
            r.tok[...], r.w[:, i * LANES : (i + 1) * LANES], preferred_element_type=F32
        )
        top, bottom = part[: T // 2], part[T // 2 :]
        r.bx[2 * i] = jnp.where(lane < Q, top, pltpu.roll(bottom, Q, 1)).astype(BF16)
        r.bx[2 * i + 1] = jnp.where(lane < Q, pltpu.roll(top, Q, 1), bottom).astype(BF16)

    total = r.rx[z]
    for k, copy in rz1:
        copy.wait_recv()
        total = total + r.rr[k]
    r.rg[z] = (SCALE * total).astype(BF16).astype(F32)
    rz2 = [(k, send(r.rg.at[z], r.rg.at[z], "rz2", k, at(zz=zp(k)))) for k in kz]

    for _, copy in gz2:
        copy.wait_recv()
    spread_into(from_blocks(r.gg), r.spread_g)
    sib = []
    for part in range(2):
        columns = pl.ds(pl.multiple_of(other_half + part * 256, 256), 256)
        r.sx[part] = jnp.dot(r.spread_g[...], r.tok[:, columns], preferred_element_type=F32)
        sib.append(send(r.sx.at[part], r.sr.at[part], "sib", part, sibling))
    for part in range(2):
        columns = pl.ds(pl.multiple_of(half + part * 256, 256), 256)
        r.own[part] = jnp.dot(r.spread_g[...], r.tok[:, columns], preferred_element_type=F32)

    def chip_sum(part, a, hh):
        rows = slice(a * RANK, (a + 1) * RANK)
        cols = slice(hh * LANES, (hh + 1) * LANES)
        return (r.own[part, rows, cols] + r.sr[part, rows, cols]).astype(BF16)

    sib[0].wait_recv()
    for xx in range(xs):
        for yy in range(ys):
            r.a1x[xx, yy] = chip_sum(0, yy * ms + xx // 2, xx % 2)
    a1 = [(k, send(r.a1x.at[xp(k)], r.a1r.at[k], "a1", k, at(xx=xp(k)))) for k in kx]

    for _, copy in rz2:
        copy.wait_recv()
    spread_into(from_blocks(r.rg), r.spread_r)
    cot2 = jnp.concatenate([r.cot[...], r.cot[...]], axis=0)
    grad_b = lax.dot_general(
        r.spread_r[...], cot2, (((1,), (1,)), ((), ())), preferred_element_type=F32
    )
    lane16 = lax.broadcasted_iota(jnp.int32, (RANK, LANES), 1)
    for yy in range(ys):
        for s in range(nb):
            row = (yy * ms + 2 * s) * RANK
            r.sbx[yy, s] = jnp.where(
                lane16 < Q, grad_b[row : row + RANK], grad_b[row + RANK : row + 2 * RANK]
            )
    sib.append(send(r.sbx, r.sbr, "sib", 2, sibling))

    sib[1].wait_recv()
    for yy in range(ys):
        for xx in range(xs):
            r.b1x[yy, xx] = chip_sum(1, yy * ms + xx // 2, xx % 2)
    sib[2].wait_recv()
    for yy in range(ys):
        for s in range(nb):
            r.b1x[yy, xs + s] = (r.sbx[yy, s] + r.sbr[yy, s]).astype(BF16)
    b1 = [(k, send(r.b1x.at[yp(k)], r.b1r.at[k], "b1", k, at(yy=yp(k)))) for k in ky]

    base = [(k, send(r.bx.at[zp(k)], r.br.at[k], "bz", k, at(zz=zp(k)))) for k in kz]

    cc.wait_recv()
    r.c1[...] = r.c0[...] + r.c0r[...]
    cx = [(k, send(r.c1, r.c1r.at[k], "cx", k, at(xx=xp(k)))) for k in kx]
    total = r.c1[...]
    for k, copy in cx:
        copy.wait_recv()
        total = total + r.c1r[k]
    r.c2[...] = total
    cy = [(k, send(r.c2, r.c2r.at[k], "cy", k, at(yy=yp(k)))) for k in ky]

    for _, copy in a1:
        copy.wait_recv()
    for yy in range(ys):
        total = r.a1x[x, yy].astype(F32)
        for k in kx:
            total = total + r.a1r[k, yy].astype(F32)
        r.a2x[yy] = total
    a2 = [(k, send(r.a2x.at[yp(k)], r.a2r.at[k], "a2", k, at(yy=yp(k)))) for k in ky]
    for _, copy in b1:
        copy.wait_recv()
    sums = []
    for s in range(xs + nb):
        total = r.b1x[y, s].astype(F32)
        for k in ky:
            total = total + r.b1r[k, s].astype(F32)
        sums.append(total)
    for xx in range(xs):
        r.b2x[xx, 0] = sums[xx]
        r.b2x[xx, 1] = sums[xs + xx // 4]
    b2 = [(k, send(r.b2x.at[xp(k)], r.b2r.at[k], "b2", k, at(xx=xp(k)))) for k in kx]

    total = r.c2[...]
    for k, copy in cy:
        copy.wait_recv()
        total = total + r.c2r[k]
    lane8 = lax.broadcasted_iota(jnp.int32, (8, LANES), 1)
    count = jnp.sum(jnp.where(lane8 == y * ms + m, total, 0.0), axis=1, keepdims=True)
    count16 = jnp.concatenate([jnp.broadcast_to(count, (8, LANES))] * 2, axis=0)
    r.pfr[q] = r.pfx[q]
    for copy in pf:
        copy.wait_recv()

    def unit(i, part):
        cols = slice(part * LANES, (part + 1) * LANES)
        return jnp.concatenate([r.pfr[j, i, :, cols] for j in range(4)], axis=0)

    def update_unit(part, total):
        gradient = total * SCALE / count16
        for j in range(4):
            r.g4[j, :, part * LANES : (part + 1) * LANES] = gradient[4 * j : 4 * j + 4]
        new_master, _, _ = adam_step(unit(0, part), unit(1, part), unit(2, part), gradient)
        columns = pl.ds(pl.multiple_of(half + part * 256 + h * LANES, LANES), LANES)
        r.rows[y, m, :, columns] = new_master.astype(BF16)

    cols_a = pl.ds(pl.multiple_of(half + h * LANES, LANES), LANES)
    cols_b = pl.ds(pl.multiple_of(half + 256 + h * LANES, LANES), LANES)
    wide_b = pl.ds(pl.multiple_of(half + 256, 256), 256)

    total = r.a2x[y]
    for k, copy in a2:
        copy.wait_recv()
        total = total + r.a2r[k]
    update_unit(0, total)
    tile = r.rows.at[y, m, :, cols_a]
    ay = [(k, send(tile, tile, "ay", k, at(yy=yp(k)))) for k in ky]

    total = r.b2x[x, 0]
    total_b = r.b2x[x, 1]
    for k, copy in b2:
        copy.wait_recv()
        total = total + r.b2r[k, 0]
        total_b = total_b + r.b2r[k, 1]
    update_unit(1, total)
    tile = r.rows.at[y, m, :, cols_b]
    bx_ = [(k, send(tile, tile, "bx_", k, at(xx=xp(k)))) for k in kx]

    odd = m % 2
    for j in range(4):
        r.bq[j] = jnp.where(
            odd == 1, total_b[4 * j : 4 * j + 4, Q:], total_b[4 * j : 4 * j + 4, :Q]
        )
    gradient = 0.25 * r.bq[q] / count16[:4, :Q]
    new_master, new_first, new_second = adam_step(r.mb[...], r.fb_[...], r.sb[...], gradient)
    r.nmb[...] = new_master
    r.nfb[...] = new_first
    r.nsb[...] = new_second
    wide = jnp.concatenate([new_master, new_master], axis=1)
    lane4 = lax.broadcasted_iota(jnp.int32, (4, LANES), 1)
    wide = jnp.where((lane4 // Q) == odd, wide, 0.0)
    r.bg[x] = jnp.concatenate([jnp.where(q == j, wide, 0.0) for j in range(4)], axis=0).astype(BF16)
    bbx = [(k, send(r.bg.at[x], r.bg.at[x], "bbx", k, at(xx=xp(k)))) for k in kx]

    ret = []
    for k in range(1, 4):
        hk, ck = k // 2, k % 2
        h2 = h + hk - 2 * h * hk
        c2 = core + ck - 2 * core * ck
        ret.append(
            send(r.g4.at[2 * h2 + c2], r.g4r.at[q], "ret", k, at(xx=2 * m + h2, cc=c2))
        )

    for _, copy in ay:
        copy.wait_recv()
    column_a = r.rows.at[:, m, :, cols_a]
    ax = [(k, send(column_a, column_a, "ax", k, at(xx=xp(k)))) for k in kx]
    fa = [send(column_a, column_a, "fa", 0, sibling)]
    for _, copy in bx_:
        copy.wait_recv()
    row_b = r.rows.at[y, :, :, wide_b]
    by = [(k, send(row_b, row_b, "by", k, at(yy=yp(k)))) for k in ky]
    fb = [send(row_b, row_b, "fb", 0, sibling)]
    for _, copy in bbx:
        copy.wait_recv()
    for s in range(nb):
        total = r.bg[4 * s].astype(F32)
        for i in range(1, 4):
            total = total + r.bg[4 * s + i].astype(F32)
        r.bt[y, s] = total.astype(BF16)
    bby = [(k, send(r.bt.at[y], r.bt.at[y], "bby", k, at(yy=yp(k)))) for k in ky]

    r.g4r[q] = r.g4[q]
    for copy in ret:
        copy.wait_recv()
    for j in range(4):
        hj, cj = j // 2, j % 2
        for part in range(2):
            col = cj * (D // 2) + part * 256 + hj * LANES
            cols = slice(col, col + LANES)
            new_master, new_first, new_second = adam_step(
                r.ma[:, cols],
                r.fa_[:, cols],
                r.sa[:, cols],
                r.g4r[j, :, part * LANES : (part + 1) * LANES],
            )
            r.nma[:, cols] = new_master
            r.nfa[:, cols] = new_first
            r.nsa[:, cols] = new_second

    term = jnp.dot(r.up[...], r.spread_r[...], preferred_element_type=F32)
    total = r.bx[z].astype(F32)
    for k, copy in base:
        copy.wait_recv()
        total = total + r.br[k].astype(F32)
    turned = jnp.transpose(total)
    r.mixed[:, : T // 2] = (turned[:Q] + 0.25 * term[:, : T // 2]).astype(BF16)
    r.mixed[:, T // 2 :] = (turned[Q:] + 0.25 * term[:, T // 2 :]).astype(BF16)

    for k, copy in ax:
        copy.wait_recv()
        source = from_x(k)
        region = r.rows.at[
            :,
            source // 2,
            :,
            pl.ds(pl.multiple_of(half + (source % 2) * LANES, LANES), LANES),
        ]
        fa.append(send(region, region, "fa", k, sibling))
    for k, copy in by:
        copy.wait_recv()
        region = r.rows.at[from_y(k), :, :, wide_b]
        fb.append(send(region, region, "fb", k, sibling))
    for _, copy in bby:
        copy.wait_recv()
    bbs = send(r.bt, r.bs, "bbs", 0, sibling)
    for copy in fa + fb:
        copy.wait_recv()
    out = pltpu.make_async_copy(r.rows, r.reta, r.out_s.at[0])
    out.start()
    bbs.wait_recv()
    for yy in range(ys):
        for s in range(nb):
            both = r.bt[yy, s].astype(F32) + r.bs[yy, s].astype(F32)
            row = (yy * ms + 2 * s) * RANK
            r.ball[row : row + RANK, :] = both
            r.ball[row + RANK : row + 2 * RANK, :] = pltpu.roll(both, Q, 1)
    r.retb[...] = jnp.transpose(r.ball[...])[:Q].astype(BF16)
    out.wait()
    for copy in started:
        copy.wait_send()


def shards(ys, xs, zs, tok, w, down, up, cot, idx, ma, mb, fa, sa, fb, sb):
    ms = xs // 2
    c_rows = ys * ms * RANK
    order, shapes = scratch(ys, xs, zs)
    vmem = pl.BlockSpec(memory_space=pltpu.VMEM)
    hbm = pl.BlockSpec(memory_space=pl.ANY)
    own = jax.ShapeDtypeStruct((4, D), F32)
    own_b = jax.ShapeDtypeStruct((4, Q), F32)
    out = pl.pallas_call(
        functools.partial(kernel, ys, xs, zs, order),
        out_shape=(
            jax.ShapeDtypeStruct((Q, T), BF16),
            own,
            own_b,
            own,
            own,
            own_b,
            own_b,
            jax.ShapeDtypeStruct((ys, ms, RANK, D), BF16),
            jax.ShapeDtypeStruct((Q, c_rows), BF16),
        ),
        in_specs=[hbm] * 3 + [vmem] * 9,
        out_specs=(vmem,) * 7 + (hbm, vmem),
        scratch_shapes=shapes,
        compiler_params=pltpu.CompilerParams(
            collective_id=0, has_side_effects=True, vmem_limit_bytes=56 * 1024 * 1024
        ),
    )(tok, w, down, up.T, cot.T, idx.T, ma, mb, fa, sa, fb, sb)
    mixed, nma, nmb, nfa, nsa, nfb, nsb, reta, retb = out
    return (mixed.T, nma, nmb, nfa, nsa, nfb, nsb, reta.reshape(c_rows, D), retb.T)


def build(mesh, ys, xs, zs):
    both, width = P("dp", "fsdp"), P(None, "fsdp")
    return jax.shard_map(
        functools.partial(shards, ys, xs, zs),
        mesh=mesh,
        in_specs=(both, P("fsdp", None), width, width, both, P("dp", None)) + (both,) * 6,
        out_specs=(both,) * 7 + (width, width),
        check_vma=False,
    )


def solution(mesh):
    return build(mesh, YS, XS, ZS)
```

```python
import functools
from itertools import zip_longest

import jax
import jax.numpy as jnp
from jax import lax
from jax.experimental import pallas as pl
from jax.experimental.pallas import tpu as pltpu
from jax.sharding import PartitionSpec as P

YS, XS, ZS = 8, 8, 8
MODEL_WIDTH = 8192
RANK = 16
STEP = 10
BETA_ONE = 0.9
BETA_TWO = 0.999
ADAM_EPS = 1e-08
LEARN_RATE = 0.01
SCALE = 1.0 / MODEL_WIDTH**0.5

MESH = pl.DeviceIdType.MESH
F32 = jnp.float32
BF16 = jnp.bfloat16
T = 512
D = 1024
Q = 64
LANES = 128


def adam_step(master, moment_one, moment_two, gradient):
    new_one = BETA_ONE * moment_one + (1.0 - BETA_ONE) * gradient
    new_two = BETA_TWO * moment_two + (1.0 - BETA_TWO) * gradient * gradient
    fix_one = 1.0 - BETA_ONE**STEP
    fix_two = 1.0 - BETA_TWO**STEP
    update = new_one / fix_one / (jnp.sqrt(new_two / fix_two) + ADAM_EPS)
    return (master - LEARN_RATE * update, new_one, new_two)


def far_first(n):
    return sorted(range(1, n), key=lambda k: -min(k, n - k))


def scratch(ys, xs, zs):
    ms = xs // 2
    nb = ms // 2
    c = ys * ms * RANK
    bz = 8 // zs
    v = pltpu.VMEM
    dma = pltpu.SemaphoreType.DMA
    bufs = dict(
        tok=v((T, D), BF16),
        down=v((c, D), BF16),
        w=v((D, zs * Q), BF16),
        up=v((Q, c), BF16),
        cot=v((Q, T), BF16),
        idx=v((1, T), jnp.int32),
        ma=v((4, D), F32),
        fa_=v((4, D), F32),
        sa=v((4, D), F32),
        mb=v((4, Q), F32),
        fb_=v((4, Q), F32),
        sb=v((4, Q), F32),
        proj=v((c, T), F32),
        spread_r=v((c, T), BF16),
        spread_g=v((c, T), BF16),
        gx=v((zs, bz * 8, LANES), F32),
        gr=v((zs, bz * 8, LANES), F32),
        gg=v((zs, bz * 8, LANES), F32),
        rx=v((zs, bz * 8, LANES), F32),
        rr=v((zs, bz * 8, LANES), F32),
        rg=v((zs, bz * 8, LANES), F32),
        bx=v((zs, T // 2, LANES), BF16),
        br=v((zs, T // 2, LANES), BF16),
        c0=v((8, LANES), F32),
        c0r=v((8, LANES), F32),
        c1=v((8, LANES), F32),
        c1r=v((xs, 8, LANES), F32),
        c2=v((8, LANES), F32),
        c2r=v((ys, 8, LANES), F32),
        pfx=v((4, 3, 4, 256), F32),
        pfr=v((4, 3, 4, 256), F32),
        sx=v((2, c, 256), F32),
        sr=v((2, c, 256), F32),
        own=v((2, c, 256), F32),
        sbx=v((ys, nb, RANK, LANES), F32),
        sbr=v((ys, nb, RANK, LANES), F32),
        a1x=v((xs, ys, RANK, LANES), BF16),
        a1r=v((xs, ys, RANK, LANES), BF16),
        a2x=v((ys, RANK, LANES), F32),
        a2r=v((ys, RANK, LANES), F32),
        b1x=v((ys, xs, RANK, LANES), BF16),
        b1r=v((ys, xs, RANK, LANES), BF16),
        b2x=v((xs, RANK, LANES), F32),
        b2r=v((xs, RANK, LANES), F32),
        u1x=v((ys, nb, RANK, LANES), BF16),
        u1r=v((ys, nb, RANK, LANES), BF16),
        u2x=v((nb, RANK, LANES), F32),
        u2r=v((xs, RANK, LANES), F32),
        g4=v((4, 4, 256), F32),
        g4r=v((4, 4, 256), F32),
        bq=v((4, 4, Q), F32),
        bg=v((xs, RANK, LANES), BF16),
        bt=v((ys, nb, RANK, LANES), BF16),
        bs=v((ys, nb, RANK, LANES), BF16),
        ball=v((c, LANES), F32),
    )
    sems = dict(
        load=12, gz1=zs, gz2=zs, rz1=zs, rz2=zs, bz=zs, cc=1, cx=xs, cy=ys, pf=4, sib=3,
        a1=2 * xs, b1=2 * ys, a2=ys, b2=xs, u1=ys, u2=xs, ret=4, ay=ys, ax=xs * (ys // 2),
        bx_=xs, by=ys * ms, bbx=xs, bby=ys, bbs=1,
        fa=xs, fb=ys,
    )
    local = ("load",)
    order = list(bufs)
    shapes = list(bufs.values())
    for name, n in sems.items():
        order.append(name + "_s")
        shapes.append(dma((n,)))
        if name not in local:
            order.append(name + "_r")
            shapes.append(dma((n,)))
    return order, shapes


INPUTS = ("tok", "w", "down", "up", "cot", "idx", "ma", "mb", "fa_", "sa", "fb_", "sb")
LOADS = ("up", "cot", "idx", "down", "tok", "w", "ma", "fa_", "sa", "mb", "fb_", "sb")
OUTPUTS = ("mixed", "nma", "nmb", "nfa", "nsa", "nfb", "nsb", "reta", "retb")


class Refs:
    def __init__(self, names, refs):
        self.__dict__.update(zip(names, refs))


def kernel(ys, xs, zs, order, *refs):
    hbm = dict(zip(INPUTS, refs))
    r = Refs(OUTPUTS + tuple(order), refs[len(INPUTS) :])
    ms = xs // 2
    nb = ms // 2
    na = ys * ms
    c_rows = na * RANK
    bz = 8 // zs
    dp, z = lax.axis_index("dp"), lax.axis_index("fsdp")
    core = dp % 2
    x = (dp // 2) % xs
    y = dp // (2 * xs)
    h, m = x % 2, x // 2
    q = 2 * h + core
    half = core * (D // 2)
    other_half = (1 - core) * (D // 2)

    def at(yy=None, xx=None, cc=None, zz=None):
        yy = y if yy is None else yy
        xx = x if xx is None else xx
        cc = core if cc is None else cc
        return ((yy * xs + xx) * 2 + cc, z if zz is None else zz)

    started = []

    def send(src, dst, name, slot, device):
        copy = pltpu.make_async_remote_copy(
            src_ref=src,
            dst_ref=dst,
            send_sem=getattr(r, name + "_s").at[slot],
            recv_sem=getattr(r, name + "_r").at[slot],
            device_id=device,
            device_id_type=MESH,
        )
        copy.start()
        started.append(copy)
        return copy

    def xp(k):
        return lax.rem(x + k, xs)

    def yp(k):
        return lax.rem(y + k, ys)

    def zp(k):
        return lax.rem(z + k, zs)

    def from_x(k):
        return lax.rem(x + xs - k, xs)

    def from_y(k):
        return lax.rem(y + ys - k, ys)

    sibling = at(cc=1 - core)
    kx, ky, kz = far_first(xs), far_first(ys), far_first(zs)

    loads = {}
    for i, name in enumerate(LOADS):
        loads[name] = pltpu.make_async_copy(hbm[name], getattr(r, name), r.load_s.at[i])
        if i < 3:
            loads[name].start()

    barrier = pltpu.get_barrier_semaphore()
    partners = [at(zz=zp(k)) for k in kz] + [at(xx=xp(k)) for k in kx] + [at(yy=yp(k)) for k in ky]
    x_pair = x + 1 - 2 * h
    partners += [sibling, at(xx=x_pair, cc=1 - core)]
    for device in partners:
        pl.semaphore_signal(barrier, inc=1, device_id=device, device_id_type=MESH)

    for name in LOADS[3:]:
        loads[name].start()
    for name in ("up", "cot", "idx"):
        loads[name].wait()
    idx = r.idx[...]
    idx16 = jnp.broadcast_to(idx, (RANK, T))

    def chosen(values):
        total = jnp.zeros((RANK, T), F32)
        for a in range(na):
            total = jnp.where(idx16 == a, values[a * RANK : (a + 1) * RANK, :], total)
        return total

    def to_blocks(values, ref):
        for b in range(8):
            kh, tb = b // 4, b % 4
            ref[b // bz, (b % bz) * 8 : (b % bz) * 8 + 8, :] = values[
                kh * 8 : kh * 8 + 8, tb * LANES : (tb + 1) * LANES
            ]

    def from_blocks(ref):
        halves = []
        for kh in range(2):
            parts = []
            for tb in range(4):
                b = kh * 4 + tb
                parts.append(ref[b // bz, (b % bz) * 8 : (b % bz) * 8 + 8, :])
            halves.append(jnp.concatenate(parts, axis=1))
        return jnp.concatenate(halves, axis=0)

    def spread_into(values, ref):
        for a in range(na):
            ref[a * RANK : (a + 1) * RANK, :] = jnp.where(idx16 == a, values, 0.0).astype(BF16)

    r.proj[...] = lax.dot_general(
        r.up[...], r.cot[...], (((0,), (0,)), ((), ())), preferred_element_type=F32
    )
    to_blocks(chosen(r.proj), r.gx)
    pl.semaphore_wait(barrier, len(partners))

    gz1 = [(k, send(r.gx.at[zp(k)], r.gr.at[k], "gz1", k, at(zz=zp(k)))) for k in kz]
    ids = lax.broadcasted_iota(jnp.int32, (LANES, T), 0)
    onehot = jnp.where(ids == jnp.broadcast_to(idx, (LANES, T)), 1.0, 0.0).astype(BF16)
    counts = lax.dot_general(
        jnp.ones((8, T), BF16), onehot, (((1,), (1,)), ((), ())), preferred_element_type=F32
    )
    r.c0[...] = counts
    cc = send(r.c0, r.c0r, "cc", 0, sibling)
    loads["down"].wait()
    loads["tok"].wait()
    r.proj[...] = lax.dot_general(
        r.down[...], r.tok[...], (((1,), (1,)), ((), ())), preferred_element_type=F32
    )
    to_blocks(chosen(r.proj), r.rx)
    rz1 = [(k, send(r.rx.at[zp(k)], r.rr.at[k], "rz1", k, at(zz=zp(k)))) for k in kz]

    total = r.gx[z]
    for k, copy in gz1:
        copy.wait_recv()
        total = total + r.gr[k]
    r.gg[z] = (0.25 * total).astype(BF16).astype(F32)
    gz2 = [(k, send(r.gg.at[z], r.gg.at[z], "gz2", k, at(zz=zp(k)))) for k in kz]

    loads["w"].wait()
    lane = lax.broadcasted_iota(jnp.int32, (T // 2, LANES), 1)
    for i in range(zs // 2):
        part = jnp.dot(
            r.tok[...], r.w[:, i * LANES : (i + 1) * LANES], preferred_element_type=F32
        )
        top, bottom = part[: T // 2], part[T // 2 :]
        r.bx[2 * i] = jnp.where(lane < Q, top, pltpu.roll(bottom, Q, 1)).astype(BF16)
        r.bx[2 * i + 1] = jnp.where(lane < Q, pltpu.roll(top, Q, 1), bottom).astype(BF16)

    total = r.rx[z]
    for k, copy in rz1:
        copy.wait_recv()
        total = total + r.rr[k]
    r.rg[z] = (SCALE * total).astype(BF16).astype(F32)
    rz2 = [(k, send(r.rg.at[z], r.rg.at[z], "rz2", k, at(zz=zp(k)))) for k in kz]

    for name in ("ma", "fa_", "sa", "mb", "fb_", "sb"):
        loads[name].wait()
    for j in range(4):
        hj, cj = j // 2, j % 2
        for i, ref in enumerate((r.ma, r.fa_, r.sa)):
            col = cj * (D // 2) + hj * LANES
            r.pfx[j, i, :, 0:LANES] = ref[:, col : col + LANES]
            r.pfx[j, i, :, LANES : 2 * LANES] = ref[:, col + 256 : col + 256 + LANES]
    pf = []
    for k in range(1, 4):
        hk, ck = k // 2, k % 2
        h2 = h + hk - 2 * h * hk
        c2 = core + ck - 2 * core * ck
        pf.append(
            send(
                r.pfx.at[2 * h2 + c2], r.pfr.at[q], "pf", k, at(xx=2 * m + h2, cc=c2)
            )
        )

    for _, copy in gz2:
        copy.wait_recv()
    spread_into(from_blocks(r.gg), r.spread_g)
    sib = []
    for part in range(2):
        columns = pl.ds(pl.multiple_of(other_half + part * 256, 256), 256)
        r.sx[part] = jnp.dot(r.spread_g[...], r.tok[:, columns], preferred_element_type=F32)
        sib.append(send(r.sx.at[part], r.sr.at[part], "sib", part, sibling))
    for part in range(2):
        columns = pl.ds(pl.multiple_of(half + part * 256, 256), 256)
        r.own[part] = jnp.dot(r.spread_g[...], r.tok[:, columns], preferred_element_type=F32)

    def chip_sum(part, yy, xx):
        rows = pl.ds(pl.multiple_of((yy * ms + xx // 2) * RANK, RANK), RANK)
        cols = pl.ds(pl.multiple_of((xx % 2) * LANES, LANES), LANES)
        return (r.own[part, rows, cols] + r.sr[part, rows, cols]).astype(BF16)

    oy, ox = ky + [0], kx + [0]
    cuts_y = (slice(0, max(1, 3 * ys // 8)), slice(max(1, 3 * ys // 8), ys))
    cuts_x = (slice(0, max(1, 3 * xs // 8)), slice(max(1, 3 * xs // 8), xs))
    sib[0].wait_recv()
    a1 = []
    for g, group in enumerate(cuts_y):
        for i in range(group.start, group.stop):
            for xx in range(xs):
                r.a1x[xx, i] = chip_sum(0, yp(oy[i]), xx)
        for k in kx:
            src, dst = r.a1x.at[xp(k), group], r.a1r.at[k, group]
            a1.append(send(src, dst, "a1", g * xs + k, at(xx=xp(k))))
    sib[1].wait_recv()
    b1 = []
    for g, group in enumerate(cuts_x):
        for i in range(group.start, group.stop):
            for yy in range(ys):
                r.b1x[yy, i] = chip_sum(1, yy, xp(ox[i]))
        for k in ky:
            src, dst = r.b1x.at[yp(k), group], r.b1r.at[k, group]
            b1.append(send(src, dst, "b1", g * ys + k, at(yy=yp(k))))

    for _, copy in rz2:
        copy.wait_recv()
    spread_into(from_blocks(r.rg), r.spread_r)
    cot2 = jnp.concatenate([r.cot[...], r.cot[...]], axis=0)
    grad_b = lax.dot_general(
        r.spread_r[...], cot2, (((1,), (1,)), ((), ())), preferred_element_type=F32
    )
    lane16 = lax.broadcasted_iota(jnp.int32, (RANK, LANES), 1)
    for yy in range(ys):
        for s in range(nb):
            row = (yy * ms + 2 * s) * RANK
            r.sbx[yy, s] = jnp.where(
                lane16 < Q, grad_b[row : row + RANK], grad_b[row + RANK : row + 2 * RANK]
            )
    sib.append(send(r.sbx, r.sbr, "sib", 2, sibling))

    cc.wait_recv()
    r.c1[...] = r.c0[...] + r.c0r[...]
    cx = [(k, send(r.c1, r.c1r.at[k], "cx", k, at(xx=xp(k)))) for k in kx]
    sib[2].wait_recv()
    for yy in range(ys):
        for s in range(nb):
            r.u1x[yy, s] = (r.sbx[yy, s] + r.sbr[yy, s]).astype(BF16)
    u1 = [(k, send(r.u1x.at[yp(k)], r.u1r.at[k], "u1", k, at(yy=yp(k)))) for k in ky]

    base = [(k, send(r.bx.at[zp(k)], r.br.at[k], "bz", k, at(zz=zp(k)))) for k in kz]

    total = r.c1[...]
    for k, copy in cx:
        copy.wait_recv()
        total = total + r.c1r[k]
    r.c2[...] = total
    cy = [(k, send(r.c2, r.c2r.at[k], "cy", k, at(yy=yp(k)))) for k in ky]

    a2, b2 = [], []
    for g in range(2):
        for copy in a1[g * len(kx) : (g + 1) * len(kx)]:
            copy.wait_recv()
        for i in range(cuts_y[g].start, cuts_y[g].stop):
            total = r.a1x[x, i].astype(F32)
            for k in kx:
                total = total + r.a1r[k, i].astype(F32)
            r.a2x[i] = total
            k = oy[i]
            if k:
                a2.append((k, send(r.a2x.at[i], r.a2r.at[k], "a2", k, at(yy=yp(k)))))
        for copy in b1[g * len(ky) : (g + 1) * len(ky)]:
            copy.wait_recv()
        for i in range(cuts_x[g].start, cuts_x[g].stop):
            total = r.b1x[y, i].astype(F32)
            for k in ky:
                total = total + r.b1r[k, i].astype(F32)
            r.b2x[i] = total
            k = ox[i]
            if k:
                b2.append((k, send(r.b2x.at[i], r.b2r.at[k], "b2", k, at(xx=xp(k)))))
    for _, copy in u1:
        copy.wait_recv()
    for s in range(nb):
        total = r.u1x[y, s].astype(F32)
        for k in ky:
            total = total + r.u1r[k, s].astype(F32)
        r.u2x[s] = total
    u2 = [(k, send(r.u2x.at[xp(k) // 4], r.u2r.at[k], "u2", k, at(xx=xp(k)))) for k in kx]

    total = r.c2[...]
    for k, copy in cy:
        copy.wait_recv()
        total = total + r.c2r[k]
    lane8 = lax.broadcasted_iota(jnp.int32, (8, LANES), 1)
    count = jnp.sum(jnp.where(lane8 == y * ms + m, total, 0.0), axis=1, keepdims=True)
    count16 = jnp.concatenate([jnp.broadcast_to(count, (8, LANES))] * 2, axis=0)
    r.pfr[q] = r.pfx[q]
    for copy in pf:
        copy.wait_recv()

    def unit(i, part):
        cols = slice(part * LANES, (part + 1) * LANES)
        return jnp.concatenate([r.pfr[j, i, :, cols] for j in range(4)], axis=0)

    def update_unit(part, total):
        gradient = total * SCALE / count16
        for j in range(4):
            r.g4[j, :, part * LANES : (part + 1) * LANES] = gradient[4 * j : 4 * j + 4]
        new_master, _, _ = adam_step(unit(0, part), unit(1, part), unit(2, part), gradient)
        columns = pl.ds(pl.multiple_of(half + part * 256 + h * LANES, LANES), LANES)
        r.reta[y, m, :, columns] = new_master.astype(BF16)

    cols_a = pl.ds(pl.multiple_of(half + h * LANES, LANES), LANES)
    cols_b = pl.ds(pl.multiple_of(half + 256 + h * LANES, LANES), LANES)
    wide_b = pl.ds(pl.multiple_of(half + 256, 256), 256)

    total = r.a2x[ys - 1]
    for k, copy in a2:
        copy.wait_recv()
        total = total + r.a2r[k]
    update_unit(0, total)
    tile = r.reta.at[y, m, :, cols_a]
    ay = [(k, send(tile, tile, "ay", k, at(yy=yp(k)))) for k in ky]

    total = r.b2x[xs - 1]
    for k, copy in b2:
        copy.wait_recv()
        total = total + r.b2r[k]
    update_unit(1, total)
    tile = r.reta.at[y, m, :, cols_b]
    bx_ = [(k, send(tile, tile, "bx_", k, at(xx=xp(k)))) for k in kx]

    odd = m % 2
    total_b = r.u2x[x // 4]
    for k, copy in u2:
        copy.wait_recv()
        total_b = total_b + r.u2r[k]
    for j in range(4):
        r.bq[j] = jnp.where(
            odd == 1, total_b[4 * j : 4 * j + 4, Q:], total_b[4 * j : 4 * j + 4, :Q]
        )
    gradient = 0.25 * r.bq[q] / count16[:4, :Q]
    new_master, new_first, new_second = adam_step(r.mb[...], r.fb_[...], r.sb[...], gradient)
    r.nmb[...] = new_master
    r.nfb[...] = new_first
    r.nsb[...] = new_second
    wide = jnp.concatenate([new_master, new_master], axis=1)
    lane4 = lax.broadcasted_iota(jnp.int32, (4, LANES), 1)
    wide = jnp.where((lane4 // Q) == odd, wide, 0.0)
    r.bg[x] = jnp.concatenate([jnp.where(q == j, wide, 0.0) for j in range(4)], axis=0).astype(BF16)
    bbx = [(k, send(r.bg.at[x], r.bg.at[x], "bbx", k, at(xx=xp(k)))) for k in kx]

    ret = []
    for k in range(1, 4):
        hk, ck = k // 2, k % 2
        h2 = h + hk - 2 * h * hk
        c2 = core + ck - 2 * core * ck
        ret.append(
            send(r.g4.at[2 * h2 + c2], r.g4r.at[q], "ret", k, at(xx=2 * m + h2, cc=c2))
        )

    def pairs(me, count):
        step = 2 * (me % 2) - 1
        offsets = {4: (0, step, -step, 2), 2: (0, 1), 1: (0,)}[count]
        return [lax.rem(me // 2 + o + count, count) for o in offsets]

    def arrived(name, tile, me, source, n, device):
        slot = lax.rem(me - source + n, n)
        pltpu.make_async_remote_copy(
            src_ref=tile,
            dst_ref=tile,
            send_sem=getattr(r, name + "_s").at[slot],
            recv_sem=getattr(r, name + "_r").at[slot],
            device_id=device,
            device_id_type=MESH,
        ).wait_recv()

    column_a = r.reta.at[:, m, :, cols_a]
    row_b = r.reta.at[y, :, :, wide_b]
    tile_a, tile_b = r.reta.at[y, m, :, cols_a], r.reta.at[y, m, :, cols_b]
    ax, by = [], []
    for j, (pa, pb) in enumerate(zip_longest(pairs(y, ys // 2), pairs(x, ms))):
        if pa is not None:
            for source in [2 * pa, 2 * pa + 1] if j else [2 * pa + 1 - y % 2]:
                arrived("ay", tile_a, y, source, ys, at(yy=source))
            region = r.reta.at[pl.ds(2 * pa, 2), m, :, cols_a]
            for k in kx:
                ax.append((k, send(region, region, "ax", j * xs + k, at(xx=xp(k)))))
        if pb is not None:
            for source in [2 * pb, 2 * pb + 1] if j else [2 * pb + 1 - x % 2]:
                arrived("bx_", tile_b, x, source, xs, at(xx=source))
            region = r.reta.at[y, pb, :, wide_b]
            for k in ky:
                by.append((k, send(region, region, "by", j * ys + k, at(yy=yp(k)))))
    fa = [send(column_a, column_a, "fa", 0, sibling)]
    fb = [send(row_b, row_b, "fb", 0, sibling)]
    for _, copy in bbx:
        copy.wait_recv()
    for s in range(nb):
        total = r.bg[4 * s].astype(F32)
        for i in range(1, 4):
            total = total + r.bg[4 * s + i].astype(F32)
        r.bt[y, s] = total.astype(BF16)
    bby = [(k, send(r.bt.at[y], r.bt.at[y], "bby", k, at(yy=yp(k)))) for k in ky]

    r.g4r[q] = r.g4[q]
    for copy in ret:
        copy.wait_recv()
    for j in range(4):
        hj, cj = j // 2, j % 2
        for part in range(2):
            col = cj * (D // 2) + part * 256 + hj * LANES
            cols = slice(col, col + LANES)
            new_master, new_first, new_second = adam_step(
                r.ma[:, cols],
                r.fa_[:, cols],
                r.sa[:, cols],
                r.g4r[j, :, part * LANES : (part + 1) * LANES],
            )
            r.nma[:, cols] = new_master
            r.nfa[:, cols] = new_first
            r.nsa[:, cols] = new_second

    term = jnp.dot(r.up[...], r.spread_r[...], preferred_element_type=F32)
    total = r.bx[z].astype(F32)
    for k, copy in base:
        copy.wait_recv()
        total = total + r.br[k].astype(F32)
    turned = jnp.transpose(total)
    r.mixed[:, : T // 2] = (turned[:Q] + 0.25 * term[:, : T // 2]).astype(BF16)
    r.mixed[:, T // 2 :] = (turned[Q:] + 0.25 * term[:, T // 2 :]).astype(BF16)

    for k in kx:
        for other, copy in ax:
            if other == k:
                copy.wait_recv()
        source = from_x(k)
        region = r.reta.at[
            :,
            source // 2,
            :,
            pl.ds(pl.multiple_of(half + (source % 2) * LANES, LANES), LANES),
        ]
        fa.append(send(region, region, "fa", k, sibling))
    for k in ky:
        for other, copy in by:
            if other == k:
                copy.wait_recv()
        region = r.reta.at[from_y(k), :, :, wide_b]
        fb.append(send(region, region, "fb", k, sibling))
    for _, copy in bby:
        copy.wait_recv()
    bbs = send(r.bt, r.bs, "bbs", 0, sibling)
    for copy in fa + fb:
        copy.wait_recv()
    bbs.wait_recv()
    for yy in range(ys):
        for s in range(nb):
            both = r.bt[yy, s].astype(F32) + r.bs[yy, s].astype(F32)
            row = (yy * ms + 2 * s) * RANK
            r.ball[row : row + RANK, :] = both
            r.ball[row + RANK : row + 2 * RANK, :] = pltpu.roll(both, Q, 1)
    r.retb[...] = jnp.transpose(r.ball[...])[:Q].astype(BF16)
    for copy in started:
        copy.wait_send()


def place(*refs):
    sems = refs[18]
    copies = [pltpu.make_async_copy(refs[i], refs[9 + i], sems.at[i]) for i in range(9)]
    for copy in copies:
        copy.start()
    for copy in copies:
        copy.wait()


def shards(ys, xs, zs, tok, w, down, up, cot, idx, ma, mb, fa, sa, fb, sb):
    ms = xs // 2
    c_rows = ys * ms * RANK
    order, shapes = scratch(ys, xs, zs)
    vmem = pl.BlockSpec(memory_space=pltpu.VMEM)
    hbm = pl.BlockSpec(memory_space=pl.ANY)
    own, own_b = ((4, D), F32), ((4, Q), F32)
    results = (
        ((Q, T), BF16), own, own_b, own, own, own_b, own_b,
        ((ys, ms, RANK, D), BF16), ((Q, c_rows), BF16),
    )
    out = pl.pallas_call(
        functools.partial(kernel, ys, xs, zs, order),
        out_shape=tuple(pltpu.VMEM(shape, dtype) for shape, dtype in results),
        in_specs=[hbm] * 12,
        out_specs=(vmem,) * 9,
        scratch_shapes=shapes,
        compiler_params=pltpu.CompilerParams(
            collective_id=0, has_side_effects=True, vmem_limit_bytes=56 * 1024 * 1024
        ),
    )(tok, w, down, up.T, cot.T, idx.T, ma, mb, fa, sa, fb, sb)
    out = pl.pallas_call(
        place,
        out_shape=tuple(jax.ShapeDtypeStruct(shape, dtype) for shape, dtype in results),
        in_specs=[vmem] * 9,
        out_specs=(hbm,) * 9,
        scratch_shapes=[pltpu.SemaphoreType.DMA((9,))],
    )(*(pltpu.with_memory_space_constraint(o, pltpu.VMEM) for o in out))
    mixed, nma, nmb, nfa, nsa, nfb, nsb, reta, retb = out
    return (mixed.T, nma, nmb, nfa, nsa, nfb, nsb, reta.reshape(c_rows, D), retb.T)


def build(mesh, ys, xs, zs):
    both, width = P("dp", "fsdp"), P(None, "fsdp")
    return jax.shard_map(
        functools.partial(shards, ys, xs, zs),
        mesh=mesh,
        in_specs=(both, P("fsdp", None), width, width, both, P("dp", None)) + (both,) * 6,
        out_specs=(both,) * 7 + (width, width),
        check_vma=False,
    )


def solution(mesh):
    return build(mesh, YS, XS, ZS)
```

```python
import functools
from itertools import zip_longest

import jax
import jax.numpy as jnp
from jax import lax
from jax.experimental import pallas as pl
from jax.experimental.pallas import tpu as pltpu
from jax.sharding import PartitionSpec as P

YS, XS, ZS = 8, 8, 8
MODEL_WIDTH = 8192
RANK = 16
STEP = 10
BETA_ONE = 0.9
BETA_TWO = 0.999
ADAM_EPS = 1e-08
LEARN_RATE = 0.01
SCALE = 1.0 / MODEL_WIDTH**0.5

SUM_PARTS, GATHER_PARTS = 2, 2

MESH = pl.DeviceIdType.MESH
F32 = jnp.float32
BF16 = jnp.bfloat16
T = 512
D = 1024
Q = 64
LANES = 128


def adam_step(master, moment_one, moment_two, gradient):
    new_one = BETA_ONE * moment_one + (1.0 - BETA_ONE) * gradient
    new_two = BETA_TWO * moment_two + (1.0 - BETA_TWO) * gradient * gradient
    fix_one = 1.0 - BETA_ONE**STEP
    fix_two = 1.0 - BETA_TWO**STEP
    update = new_one / fix_one / (jnp.sqrt(new_two / fix_two) + ADAM_EPS)
    return (master - LEARN_RATE * update, new_one, new_two)


def far_first(n):
    return sorted(range(1, n), key=lambda k: -min(k, n - k))


def scratch(ys, xs, zs):
    ms = xs // 2
    nb = ms // 2
    c = ys * ms * RANK
    bz = 8 // zs
    v = pltpu.VMEM
    dma = pltpu.SemaphoreType.DMA
    bufs = dict(
        tok=v((T, D), BF16),
        down=v((c, D), BF16),
        w=v((D, zs * Q), BF16),
        up=v((Q, c), BF16),
        cot=v((Q, T), BF16),
        idx=v((1, T), jnp.int32),
        ma=v((4, D), F32),
        fa_=v((4, D), F32),
        sa=v((4, D), F32),
        mb=v((4, Q), F32),
        fb_=v((4, Q), F32),
        sb=v((4, Q), F32),
        proj=v((c, T), F32),
        spread_r=v((c, T), BF16),
        spread_g=v((c, T), BF16),
        gx=v((zs, bz * 8, LANES), F32),
        gr=v((zs, bz * 8, LANES), F32),
        gg=v((zs, bz * 8, LANES), F32),
        rx=v((zs, bz * 8, LANES), F32),
        rr=v((zs, bz * 8, LANES), F32),
        rg=v((zs, bz * 8, LANES), F32),
        bx=v((zs, T // 2, LANES), BF16),
        br=v((zs, T // 2, LANES), BF16),
        c0=v((8, LANES), F32),
        c0r=v((8, LANES), F32),
        c1=v((8, LANES), F32),
        c1r=v((xs, 8, LANES), F32),
        c2=v((8, LANES), F32),
        c2r=v((ys, 8, LANES), F32),
        pfx=v((4, 3, 4, 256), F32),
        pfr=v((4, 3, 4, 256), F32),
        sx=v((2, c, 256), F32),
        sr=v((2, c, 256), F32),
        own=v((2, c, 256), F32),
        sbx=v((ys, nb, RANK, LANES), F32),
        sbr=v((ys, nb, RANK, LANES), F32),
        a1x=v((xs, ys, RANK, LANES), BF16),
        a1r=v((xs, ys, RANK, LANES), BF16),
        a2x=v((ys, RANK, LANES), F32),
        a2r=v((ys, RANK, LANES), F32),
        b1x=v((ys, xs, RANK, LANES), BF16),
        b1r=v((ys, xs, RANK, LANES), BF16),
        b2x=v((xs, RANK, LANES), F32),
        b2r=v((xs, RANK, LANES), F32),
        u1x=v((ys, nb, RANK, LANES), BF16),
        u1r=v((ys, nb, RANK, LANES), BF16),
        u2x=v((nb, RANK, LANES), F32),
        u2r=v((xs, nb, RANK, LANES), F32),
        ug=v((nb, RANK, LANES), F32),
        pm=v((2, xs, 3, 4, Q), F32),
        g4=v((4, 4, 256), F32),
        g4r=v((4, 4, 256), F32),
        bq=v((4, 4, Q), F32),
        bt=v((ys, nb, RANK, LANES), BF16),
        ball=v((c, LANES), F32),
    )
    sems = dict(
        load=12, gz1=zs, gz2=zs, rz1=zs, rz2=zs, bz=zs, cc=1, cx=xs, cy=ys, pf=4, sib=3,
        a1=2 * xs, b1=2 * ys, a2=ys, b2=xs, u1=ys, u2=xs, ret=4, ay=ys, ax=xs * (ys // 2),
        bx_=xs, by=ys * ms, pm=xs, pms=1, bby=ys,
        fa=xs, fb=ys,
    )
    local = ("load",)
    order = list(bufs)
    shapes = list(bufs.values())
    for name, n in sems.items():
        order.append(name + "_s")
        shapes.append(dma((n,)))
        if name not in local:
            order.append(name + "_r")
            shapes.append(dma((n,)))
    return order, shapes


INPUTS = ("tok", "w", "down", "up", "cot", "idx", "ma", "mb", "fa_", "sa", "fb_", "sb")
LOADS = ("up", "cot", "idx", "down", "tok", "w", "ma", "fa_", "sa", "mb", "fb_", "sb")
OUTPUTS = ("mixed", "nma", "nmb", "nfa", "nsa", "nfb", "nsb", "reta", "retb")


class Refs:
    def __init__(self, names, refs):
        self.__dict__.update(zip(names, refs))


def kernel(ys, xs, zs, order, *refs):
    hbm = dict(zip(INPUTS, refs))
    r = Refs(OUTPUTS + tuple(order), refs[len(INPUTS) :])
    ms = xs // 2
    nb = ms // 2
    na = ys * ms
    c_rows = na * RANK
    bz = 8 // zs
    dp, z = lax.axis_index("dp"), lax.axis_index("fsdp")
    core = dp % 2
    x = (dp // 2) % xs
    y = dp // (2 * xs)
    h, m = x % 2, x // 2
    q = 2 * h + core
    half = core * (D // 2)
    other_half = (1 - core) * (D // 2)

    def at(yy=None, xx=None, cc=None, zz=None):
        yy = y if yy is None else yy
        xx = x if xx is None else xx
        cc = core if cc is None else cc
        return ((yy * xs + xx) * 2 + cc, z if zz is None else zz)

    started = []

    def send(src, dst, name, slot, device):
        copy = pltpu.make_async_remote_copy(
            src_ref=src,
            dst_ref=dst,
            send_sem=getattr(r, name + "_s").at[slot],
            recv_sem=getattr(r, name + "_r").at[slot],
            device_id=device,
            device_id_type=MESH,
        )
        copy.start()
        started.append(copy)
        return copy

    def xp(k):
        return lax.rem(x + k, xs)

    def yp(k):
        return lax.rem(y + k, ys)

    def zp(k):
        return lax.rem(z + k, zs)

    def from_x(k):
        return lax.rem(x + xs - k, xs)

    def from_y(k):
        return lax.rem(y + ys - k, ys)

    sibling = at(cc=1 - core)
    kx, ky, kz = far_first(xs), far_first(ys), far_first(zs)

    loads = {}
    for i, name in enumerate(LOADS):
        loads[name] = pltpu.make_async_copy(hbm[name], getattr(r, name), r.load_s.at[i])
        if i < 3:
            loads[name].start()

    barrier = pltpu.get_barrier_semaphore()
    partners = [at(zz=zp(k)) for k in kz] + [at(xx=xp(k)) for k in kx] + [at(yy=yp(k)) for k in ky]
    x_pair = x + 1 - 2 * h
    partners += [sibling, at(xx=x_pair, cc=1 - core)]
    for device in partners:
        pl.semaphore_signal(barrier, inc=1, device_id=device, device_id_type=MESH)

    for name in LOADS[3:]:
        loads[name].start()
    for name in ("up", "cot", "idx"):
        loads[name].wait()
    idx = r.idx[...]
    idx16 = jnp.broadcast_to(idx, (RANK, T))

    def chosen(values):
        total = jnp.zeros((RANK, T), F32)
        for a in range(na):
            total = jnp.where(idx16 == a, values[a * RANK : (a + 1) * RANK, :], total)
        return total

    def to_blocks(values, ref):
        for b in range(8):
            kh, tb = b // 4, b % 4
            ref[b // bz, (b % bz) * 8 : (b % bz) * 8 + 8, :] = values[
                kh * 8 : kh * 8 + 8, tb * LANES : (tb + 1) * LANES
            ]

    def from_blocks(ref):
        halves = []
        for kh in range(2):
            parts = []
            for tb in range(4):
                b = kh * 4 + tb
                parts.append(ref[b // bz, (b % bz) * 8 : (b % bz) * 8 + 8, :])
            halves.append(jnp.concatenate(parts, axis=1))
        return jnp.concatenate(halves, axis=0)

    def spread_into(values, ref):
        for a in range(na):
            ref[a * RANK : (a + 1) * RANK, :] = jnp.where(idx16 == a, values, 0.0).astype(BF16)

    r.proj[...] = lax.dot_general(
        r.up[...], r.cot[...], (((0,), (0,)), ((), ())), preferred_element_type=F32
    )
    to_blocks(chosen(r.proj), r.gx)
    pl.semaphore_wait(barrier, len(partners))

    gz1 = [(k, send(r.gx.at[zp(k)], r.gr.at[k], "gz1", k, at(zz=zp(k)))) for k in kz]
    ids = lax.broadcasted_iota(jnp.int32, (LANES, T), 0)
    onehot = jnp.where(ids == jnp.broadcast_to(idx, (LANES, T)), 1.0, 0.0).astype(BF16)
    counts = lax.dot_general(
        jnp.ones((8, T), BF16), onehot, (((1,), (1,)), ((), ())), preferred_element_type=F32
    )
    r.c0[...] = counts
    cc = send(r.c0, r.c0r, "cc", 0, sibling)
    loads["down"].wait()
    loads["tok"].wait()
    r.proj[...] = lax.dot_general(
        r.down[...], r.tok[...], (((1,), (1,)), ((), ())), preferred_element_type=F32
    )
    to_blocks(chosen(r.proj), r.rx)
    rz1 = [(k, send(r.rx.at[zp(k)], r.rr.at[k], "rz1", k, at(zz=zp(k)))) for k in kz]

    total = r.gx[z]
    for k, copy in gz1:
        copy.wait_recv()
        total = total + r.gr[k]
    r.gg[z] = (0.25 * total).astype(BF16).astype(F32)
    gz2 = [(k, send(r.gg.at[z], r.gg.at[z], "gz2", k, at(zz=zp(k)))) for k in kz]

    loads["w"].wait()
    lane = lax.broadcasted_iota(jnp.int32, (T // 2, LANES), 1)
    for i in range(zs // 2):
        part = jnp.dot(
            r.tok[...], r.w[:, i * LANES : (i + 1) * LANES], preferred_element_type=F32
        )
        top, bottom = part[: T // 2], part[T // 2 :]
        r.bx[2 * i] = jnp.where(lane < Q, top, pltpu.roll(bottom, Q, 1)).astype(BF16)
        r.bx[2 * i + 1] = jnp.where(lane < Q, pltpu.roll(top, Q, 1), bottom).astype(BF16)

    total = r.rx[z]
    for k, copy in rz1:
        copy.wait_recv()
        total = total + r.rr[k]
    r.rg[z] = (SCALE * total).astype(BF16).astype(F32)
    rz2 = [(k, send(r.rg.at[z], r.rg.at[z], "rz2", k, at(zz=zp(k)))) for k in kz]

    for name in ("ma", "fa_", "sa", "mb", "fb_", "sb"):
        loads[name].wait()
    for j in range(4):
        hj, cj = j // 2, j % 2
        for i, ref in enumerate((r.ma, r.fa_, r.sa)):
            col = cj * (D // 2) + hj * LANES
            r.pfx[j, i, :, 0:LANES] = ref[:, col : col + LANES]
            r.pfx[j, i, :, LANES : 2 * LANES] = ref[:, col + 256 : col + 256 + LANES]
    for i, ref in enumerate((r.mb, r.fb_, r.sb)):
        r.pm[core, x, i] = ref[...]
    mine = r.pm.at[core, x]
    pm = [send(mine, mine, "pm", k, at(xx=xp(k))) for k in kx]
    pf = []
    for k in range(1, 4):
        hk, ck = k // 2, k % 2
        h2 = h + hk - 2 * h * hk
        c2 = core + ck - 2 * core * ck
        pf.append(
            send(
                r.pfx.at[2 * h2 + c2], r.pfr.at[q], "pf", k, at(xx=2 * m + h2, cc=c2)
            )
        )

    for _, copy in gz2:
        copy.wait_recv()
    spread_into(from_blocks(r.gg), r.spread_g)
    sib = []
    for part in range(2):
        columns = pl.ds(pl.multiple_of(other_half + part * 256, 256), 256)
        r.sx[part] = jnp.dot(r.spread_g[...], r.tok[:, columns], preferred_element_type=F32)
        sib.append(send(r.sx.at[part], r.sr.at[part], "sib", part, sibling))
    for part in range(2):
        columns = pl.ds(pl.multiple_of(half + part * 256, 256), 256)
        r.own[part] = jnp.dot(r.spread_g[...], r.tok[:, columns], preferred_element_type=F32)

    def chip_sum(part, yy, xx):
        rows = pl.ds(pl.multiple_of((yy * ms + xx // 2) * RANK, RANK), RANK)
        cols = pl.ds(pl.multiple_of((xx % 2) * LANES, LANES), LANES)
        return (r.own[part, rows, cols] + r.sr[part, rows, cols]).astype(BF16)

    oy, ox = ky + [0], kx + [0]
    cuts_y = (slice(0, max(1, 3 * ys // 8)), slice(max(1, 3 * ys // 8), ys))
    cuts_x = (slice(0, max(1, 3 * xs // 8)), slice(max(1, 3 * xs // 8), xs))
    if SUM_PARTS == 1:
        cuts_y, cuts_x = (slice(0, ys),), (slice(0, xs),)
    sib[0].wait_recv()
    a1 = []
    for g, group in enumerate(cuts_y):
        for i in range(group.start, group.stop):
            for xx in range(xs):
                r.a1x[xx, i] = chip_sum(0, yp(oy[i]), xx)
        for k in kx:
            src, dst = r.a1x.at[xp(k), group], r.a1r.at[k, group]
            a1.append(send(src, dst, "a1", g * xs + k, at(xx=xp(k))))
    sib[1].wait_recv()
    b1 = []
    for g, group in enumerate(cuts_x):
        for i in range(group.start, group.stop):
            for yy in range(ys):
                r.b1x[yy, i] = chip_sum(1, yy, xp(ox[i]))
        for k in ky:
            src, dst = r.b1x.at[yp(k), group], r.b1r.at[k, group]
            b1.append(send(src, dst, "b1", g * ys + k, at(yy=yp(k))))

    for _, copy in rz2:
        copy.wait_recv()
    spread_into(from_blocks(r.rg), r.spread_r)
    cot2 = jnp.concatenate([r.cot[...], r.cot[...]], axis=0)
    grad_b = lax.dot_general(
        r.spread_r[...], cot2, (((1,), (1,)), ((), ())), preferred_element_type=F32
    )
    lane16 = lax.broadcasted_iota(jnp.int32, (RANK, LANES), 1)
    for yy in range(ys):
        for s in range(nb):
            row = (yy * ms + 2 * s) * RANK
            r.sbx[yy, s] = jnp.where(
                lane16 < Q, grad_b[row : row + RANK], grad_b[row + RANK : row + 2 * RANK]
            )
    sib.append(send(r.sbx, r.sbr, "sib", 2, sibling))

    cc.wait_recv()
    r.c1[...] = r.c0[...] + r.c0r[...]
    cx = [(k, send(r.c1, r.c1r.at[k], "cx", k, at(xx=xp(k)))) for k in kx]
    sib[2].wait_recv()
    for yy in range(ys):
        for s in range(nb):
            r.u1x[yy, s] = (r.sbx[yy, s] + r.sbr[yy, s]).astype(BF16)
    u1 = [(k, send(r.u1x.at[yp(k)], r.u1r.at[k], "u1", k, at(yy=yp(k)))) for k in ky]

    for copy in pm:
        copy.wait_recv()
    pms = send(r.pm.at[core], r.pm.at[core], "pms", 0, sibling)

    base = [(k, send(r.bx.at[zp(k)], r.br.at[k], "bz", k, at(zz=zp(k)))) for k in kz]

    total = r.c1[...]
    for k, copy in cx:
        copy.wait_recv()
        total = total + r.c1r[k]
    r.c2[...] = total
    cy = [(k, send(r.c2, r.c2r.at[k], "cy", k, at(yy=yp(k)))) for k in ky]

    a2, b2 = [], []
    for g in range(SUM_PARTS):
        for copy in a1[g * len(kx) : (g + 1) * len(kx)]:
            copy.wait_recv()
        for i in range(cuts_y[g].start, cuts_y[g].stop):
            total = r.a1x[x, i].astype(F32)
            for k in kx:
                total = total + r.a1r[k, i].astype(F32)
            r.a2x[i] = total
            k = oy[i]
            if k:
                a2.append((k, send(r.a2x.at[i], r.a2r.at[k], "a2", k, at(yy=yp(k)))))
        for copy in b1[g * len(ky) : (g + 1) * len(ky)]:
            copy.wait_recv()
        for i in range(cuts_x[g].start, cuts_x[g].stop):
            total = r.b1x[y, i].astype(F32)
            for k in ky:
                total = total + r.b1r[k, i].astype(F32)
            r.b2x[i] = total
            k = ox[i]
            if k:
                b2.append((k, send(r.b2x.at[i], r.b2r.at[k], "b2", k, at(xx=xp(k)))))
    for _, copy in u1:
        copy.wait_recv()
    for s in range(nb):
        total = r.u1x[y, s].astype(F32)
        for k in ky:
            total = total + r.u1r[k, s].astype(F32)
        r.u2x[s] = total
    u2 = [(k, send(r.u2x, r.u2r.at[k], "u2", k, at(xx=xp(k)))) for k in kx]

    total = r.c2[...]
    for k, copy in cy:
        copy.wait_recv()
        total = total + r.c2r[k]
    lane8 = lax.broadcasted_iota(jnp.int32, (8, LANES), 1)

    def count_of(adapter):
        count = jnp.sum(jnp.where(lane8 == y * ms + adapter, total, 0.0), axis=1, keepdims=True)
        return jnp.concatenate([jnp.broadcast_to(count, (8, LANES))] * 2, axis=0)

    count16 = count_of(m)
    count_b = [jnp.where(lane16 < Q, count_of(2 * s), count_of(2 * s + 1)) for s in range(nb)]
    pms.wait_recv()

    def side_by_side(i, s):
        halves = []
        for adapter in (2 * s, 2 * s + 1):
            rows = [r.pm[j % 2, 2 * adapter + j // 2, i] for j in range(4)]
            halves.append(jnp.concatenate(rows, axis=0))
        return jnp.concatenate(halves, axis=1)

    states_b = [[side_by_side(i, s) for i in range(3)] for s in range(nb)]
    r.pfr[q] = r.pfx[q]
    for copy in pf:
        copy.wait_recv()

    def unit(i, part):
        cols = slice(part * LANES, (part + 1) * LANES)
        return jnp.concatenate([r.pfr[j, i, :, cols] for j in range(4)], axis=0)

    def update_unit(part, total):
        gradient = total * SCALE / count16
        for j in range(4):
            r.g4[j, :, part * LANES : (part + 1) * LANES] = gradient[4 * j : 4 * j + 4]
        new_master, _, _ = adam_step(unit(0, part), unit(1, part), unit(2, part), gradient)
        columns = pl.ds(pl.multiple_of(half + part * 256 + h * LANES, LANES), LANES)
        r.reta[y, m, :, columns] = new_master.astype(BF16)

    cols_a = pl.ds(pl.multiple_of(half + h * LANES, LANES), LANES)
    cols_b = pl.ds(pl.multiple_of(half + 256 + h * LANES, LANES), LANES)
    wide_b = pl.ds(pl.multiple_of(half + 256, 256), 256)

    total = r.a2x[ys - 1]
    for k, copy in a2:
        copy.wait_recv()
        total = total + r.a2r[k]
    update_unit(0, total)
    tile = r.reta.at[y, m, :, cols_a]
    ay = [(k, send(tile, tile, "ay", k, at(yy=yp(k)))) for k in ky]

    total = r.b2x[xs - 1]
    for k, copy in b2:
        copy.wait_recv()
        total = total + r.b2r[k]
    update_unit(1, total)
    tile = r.reta.at[y, m, :, cols_b]
    bx_ = [(k, send(tile, tile, "bx_", k, at(xx=xp(k)))) for k in kx]

    sums_b = [r.u2x[s] for s in range(nb)]
    for k, copy in u2:
        copy.wait_recv()
        for s in range(nb):
            sums_b[s] = sums_b[s] + r.u2r[k, s]
    for s in range(nb):
        gradient = 0.25 * sums_b[s] / count_b[s]
        r.ug[s] = gradient
        r.bt[y, s] = adam_step(*states_b[s], gradient)[0].astype(BF16)
    bby = [(k, send(r.bt.at[y], r.bt.at[y], "bby", k, at(yy=yp(k)))) for k in ky]

    odd = m % 2
    own_b = r.ug[x // 4]
    for j in range(4):
        r.bq[j] = jnp.where(odd == 1, own_b[4 * j : 4 * j + 4, Q:], own_b[4 * j : 4 * j + 4, :Q])
    new_master, new_first, new_second = adam_step(r.mb[...], r.fb_[...], r.sb[...], r.bq[q])
    r.nmb[...] = new_master
    r.nfb[...] = new_first
    r.nsb[...] = new_second

    ret = []
    for k in range(1, 4):
        hk, ck = k // 2, k % 2
        h2 = h + hk - 2 * h * hk
        c2 = core + ck - 2 * core * ck
        ret.append(
            send(r.g4.at[2 * h2 + c2], r.g4r.at[q], "ret", k, at(xx=2 * m + h2, cc=c2))
        )

    def parts_of(me, n):
        count = min(GATHER_PARTS, n // 2)
        step = 2 * (me % 2) - 1
        offsets = {4: (0, step, -step, 2), 2: (0, 1), 1: (0,)}[count]
        return count, n // count, [lax.rem(me // (n // count) + o + count, count) for o in offsets]

    def arrived(name, tile, me, source, n, device):
        slot = lax.rem(me - source + n, n)
        pltpu.make_async_remote_copy(
            src_ref=tile,
            dst_ref=tile,
            send_sem=getattr(r, name + "_s").at[slot],
            recv_sem=getattr(r, name + "_r").at[slot],
            device_id=device,
            device_id_type=MESH,
        ).wait_recv()

    early = len(started)
    column_a = r.reta.at[:, m, :, cols_a]
    row_b = r.reta.at[y, :, :, wide_b]
    tile_a, tile_b = r.reta.at[y, m, :, cols_a], r.reta.at[y, m, :, cols_b]
    ax, by = [], []
    count_y, wide_y, order_y = parts_of(y, ys)
    count_x, wide_x, order_x = parts_of(x, xs)
    for j, (pa, pb) in enumerate(zip_longest(order_y, order_x)):
        if pa is not None:
            for i in range(1 if j == 0 else 0, wide_y):
                place = lax.rem(y + i, wide_y) if j == 0 else i
                source = wide_y * pa + place
                arrived("ay", tile_a, y, source, ys, at(yy=source))
            region = r.reta.at[pl.ds(wide_y * pa, wide_y), m, :, cols_a]
            for k in kx:
                ax.append((k, send(region, region, "ax", j * xs + k, at(xx=xp(k)))))
        if pb is not None:
            for i in range(1 if j == 0 else 0, wide_x):
                place = lax.rem(x + i, wide_x) if j == 0 else i
                source = wide_x * pb + place
                arrived("bx_", tile_b, x, source, xs, at(xx=source))
            region = r.reta.at[y, pl.ds(wide_x // 2 * pb, wide_x // 2), :, wide_b]
            for k in ky:
                by.append((k, send(region, region, "by", j * ys + k, at(yy=yp(k)))))
    fa = [send(column_a, column_a, "fa", 0, sibling)]
    fb = [send(row_b, row_b, "fb", 0, sibling)]
    r.g4r[q] = r.g4[q]
    for copy in ret:
        copy.wait_recv()
    for j in range(4):
        hj, cj = j // 2, j % 2
        for part in range(2):
            col = cj * (D // 2) + part * 256 + hj * LANES
            cols = slice(col, col + LANES)
            new_master, new_first, new_second = adam_step(
                r.ma[:, cols],
                r.fa_[:, cols],
                r.sa[:, cols],
                r.g4r[j, :, part * LANES : (part + 1) * LANES],
            )
            r.nma[:, cols] = new_master
            r.nfa[:, cols] = new_first
            r.nsa[:, cols] = new_second

    term = jnp.dot(r.up[...], r.spread_r[...], preferred_element_type=F32)
    total = r.bx[z].astype(F32)
    for k, copy in base:
        copy.wait_recv()
        total = total + r.br[k].astype(F32)
    turned = jnp.transpose(total)
    r.mixed[:, : T // 2] = (turned[:Q] + 0.25 * term[:, : T // 2]).astype(BF16)
    r.mixed[:, T // 2 :] = (turned[Q:] + 0.25 * term[:, T // 2 :]).astype(BF16)

    for copy in started[:early]:
        copy.wait_send()

    for k in kx:
        for other, copy in ax:
            if other == k:
                copy.wait_recv()
        source = from_x(k)
        region = r.reta.at[
            :,
            source // 2,
            :,
            pl.ds(pl.multiple_of(half + (source % 2) * LANES, LANES), LANES),
        ]
        fa.append(send(region, region, "fa", k, sibling))
    for k in ky:
        for other, copy in by:
            if other == k:
                copy.wait_recv()
        region = r.reta.at[from_y(k), :, :, wide_b]
        fb.append(send(region, region, "fb", k, sibling))
    for _, copy in bby:
        copy.wait_recv()
    for yy in range(ys):
        for s in range(nb):
            both = r.bt[yy, s].astype(F32)
            row = (yy * ms + 2 * s) * RANK
            r.ball[row : row + RANK, :] = both
            r.ball[row + RANK : row + 2 * RANK, :] = pltpu.roll(both, Q, 1)
    r.retb[...] = jnp.transpose(r.ball[...])[:Q].astype(BF16)
    for copy in fa + fb:
        copy.wait_recv()
    for copy in started[early:]:
        copy.wait_send()


def place(*refs):
    sems = refs[18]
    copies = [pltpu.make_async_copy(refs[i], refs[9 + i], sems.at[i]) for i in range(9)]
    for copy in copies:
        copy.start()
    for copy in copies:
        copy.wait()


def shards(ys, xs, zs, tok, w, down, up, cot, idx, ma, mb, fa, sa, fb, sb):
    ms = xs // 2
    c_rows = ys * ms * RANK
    order, shapes = scratch(ys, xs, zs)
    vmem = pl.BlockSpec(memory_space=pltpu.VMEM)
    hbm = pl.BlockSpec(memory_space=pl.ANY)
    own, own_b = ((4, D), F32), ((4, Q), F32)
    results = (
        ((Q, T), BF16), own, own_b, own, own, own_b, own_b,
        ((ys, ms, RANK, D), BF16), ((Q, c_rows), BF16),
    )
    out = pl.pallas_call(
        functools.partial(kernel, ys, xs, zs, order),
        out_shape=tuple(pltpu.VMEM(shape, dtype) for shape, dtype in results),
        in_specs=[hbm] * 12,
        out_specs=(vmem,) * 9,
        scratch_shapes=shapes,
        compiler_params=pltpu.CompilerParams(
            collective_id=0, has_side_effects=True, vmem_limit_bytes=56 * 1024 * 1024
        ),
    )(tok, w, down, up.T, cot.T, idx.T, ma, mb, fa, sa, fb, sb)
    out = pl.pallas_call(
        place,
        out_shape=tuple(jax.ShapeDtypeStruct(shape, dtype) for shape, dtype in results),
        in_specs=[vmem] * 9,
        out_specs=(hbm,) * 9,
        scratch_shapes=[pltpu.SemaphoreType.DMA((9,))],
    )(*(pltpu.with_memory_space_constraint(o, pltpu.VMEM) for o in out))
    mixed, nma, nmb, nfa, nsa, nfb, nsb, reta, retb = out
    return (mixed.T, nma, nmb, nfa, nsa, nfb, nsb, reta.reshape(c_rows, D), retb.T)


def build(mesh, ys, xs, zs):
    both, width = P("dp", "fsdp"), P(None, "fsdp")
    return jax.shard_map(
        functools.partial(shards, ys, xs, zs),
        mesh=mesh,
        in_specs=(both, P("fsdp", None), width, width, both, P("dp", None)) + (both,) * 6,
        out_specs=(both,) * 7 + (width, width),
        check_vma=False,
    )


def solution(mesh):
    return build(mesh, YS, XS, ZS)
```

```python
import functools
from itertools import zip_longest

import jax
import jax.numpy as jnp
from jax import lax
from jax.experimental import pallas as pl
from jax.experimental.pallas import tpu as pltpu
from jax.sharding import PartitionSpec as P

YS, XS, ZS = 8, 8, 8
MODEL_WIDTH = 8192
RANK = 16
STEP = 10
BETA_ONE = 0.9
BETA_TWO = 0.999
ADAM_EPS = 1e-08
LEARN_RATE = 0.01
SCALE = 1.0 / MODEL_WIDTH**0.5

SUM_PARTS, GATHER_PARTS = 2, 2

MESH = pl.DeviceIdType.MESH
F32 = jnp.float32
BF16 = jnp.bfloat16
T = 512
D = 1024
Q = 64
LANES = 128


def adam_step(master, moment_one, moment_two, gradient):
    new_one = BETA_ONE * moment_one + (1.0 - BETA_ONE) * gradient
    new_two = BETA_TWO * moment_two + (1.0 - BETA_TWO) * gradient * gradient
    fix_one = 1.0 - BETA_ONE**STEP
    fix_two = 1.0 - BETA_TWO**STEP
    update = new_one / fix_one / (jnp.sqrt(new_two / fix_two) + ADAM_EPS)
    return (master - LEARN_RATE * update, new_one, new_two)


def far_first(n):
    return sorted(range(1, n), key=lambda k: -min(k, n - k))


def scratch(ys, xs, zs):
    ms = xs // 2
    nb = ms // 2
    c = ys * ms * RANK
    bz = 8 // zs
    v = pltpu.VMEM
    dma = pltpu.SemaphoreType.DMA
    bufs = dict(
        tok=v((T, D), BF16),
        down=v((c, D), BF16),
        w=v((D, zs * Q), BF16),
        up=v((Q, c), BF16),
        cot=v((Q, T), BF16),
        idx=v((1, T), jnp.int32),
        ma=v((4, D), F32),
        fa_=v((4, D), F32),
        sa=v((4, D), F32),
        mb=v((4, Q), F32),
        fb_=v((4, Q), F32),
        sb=v((4, Q), F32),
        proj=v((c, T), F32),
        spread_r=v((c, T), BF16),
        spread_g=v((c, T), BF16),
        gx=v((zs, bz * 8, LANES), F32),
        gr=v((zs, bz * 8, LANES), F32),
        gg=v((zs, bz * 8, LANES), F32),
        rx=v((zs, bz * 8, LANES), F32),
        rr=v((zs, bz * 8, LANES), F32),
        rg=v((zs, bz * 8, LANES), F32),
        bx=v((zs, T // 2, LANES), BF16),
        br=v((zs, T // 2, LANES), BF16),
        c0=v((8, LANES), F32),
        c0r=v((8, LANES), F32),
        c1=v((8, LANES), F32),
        c1r=v((xs, 8, LANES), F32),
        c2=v((8, LANES), F32),
        c2r=v((ys, 8, LANES), F32),
        pfx=v((4, 3, 4, 256), F32),
        pfr=v((4, 3, 4, 256), F32),
        sx=v((2, c, 256), F32),
        sr=v((2, c, 256), F32),
        own=v((2, c, 256), F32),
        sbx=v((ys, nb, RANK, LANES), F32),
        sbr=v((ys, nb, RANK, LANES), F32),
        a1x=v((xs, ys, RANK, LANES), BF16),
        a1r=v((xs, ys, RANK, LANES), BF16),
        a2x=v((ys, RANK, LANES), F32),
        a2r=v((ys, RANK, LANES), F32),
        b1x=v((ys, xs, RANK, LANES), BF16),
        b1r=v((ys, xs, RANK, LANES), BF16),
        b2x=v((xs, RANK, LANES), F32),
        b2r=v((xs, RANK, LANES), F32),
        u1x=v((ys, nb, RANK, LANES), BF16),
        u1r=v((ys, nb, RANK, LANES), BF16),
        u2x=v((nb, RANK, LANES), F32),
        u2r=v((xs, nb, RANK, LANES), F32),
        ug=v((nb, RANK, LANES), F32),
        pm=v((2, xs, 3, 4, Q), F32),
        g4=v((4, 4, 256), F32),
        g4r=v((4, 4, 256), F32),
        bq=v((4, 4, Q), F32),
        bt=v((ys, nb, RANK, LANES), BF16),
        ball=v((c, LANES), F32),
    )
    sems = dict(
        load=12, gz1=zs, gz2=zs, rz1=zs, rz2=zs, bz=zs, cc=1, cx=xs, cy=ys, pf=4, sib=3,
        a1=2 * xs, b1=2 * ys, a2=ys, b2=xs, u1=ys, u2=xs, ret=4, ay=ys, ax=xs * (ys // 2),
        bx_=xs, by=ys * ms, pm=xs, pms=1, bby=ys,
        fa=xs, fb=ys,
    )
    local = ("load",)
    order = list(bufs)
    shapes = list(bufs.values())
    for name, n in sems.items():
        order.append(name + "_s")
        shapes.append(dma((n,)))
        if name not in local:
            order.append(name + "_r")
            shapes.append(dma((n,)))
    return order, shapes


INPUTS = ("tok", "w", "down", "up", "cot", "idx", "ma", "mb", "fa_", "sa", "fb_", "sb")
LOADS = ("up", "cot", "idx", "down", "tok", "w", "ma", "fa_", "sa", "mb", "fb_", "sb")
OUTPUTS = ("mixed", "nma", "nmb", "nfa", "nsa", "nfb", "nsb", "reta", "retb")


class Refs:
    def __init__(self, names, refs):
        self.__dict__.update(zip(names, refs))


def kernel(ys, xs, zs, order, *refs):
    hbm = dict(zip(INPUTS, refs))
    r = Refs(OUTPUTS + tuple(order), refs[len(INPUTS) :])
    ms = xs // 2
    nb = ms // 2
    na = ys * ms
    c_rows = na * RANK
    bz = 8 // zs
    dp, z = lax.axis_index("dp"), lax.axis_index("fsdp")
    core = dp % 2
    x = (dp // 2) % xs
    y = dp // (2 * xs)
    h, m = x % 2, x // 2
    q = 2 * h + core
    half = core * (D // 2)
    other_half = (1 - core) * (D // 2)

    def at(yy=None, xx=None, cc=None, zz=None):
        yy = y if yy is None else yy
        xx = x if xx is None else xx
        cc = core if cc is None else cc
        return ((yy * xs + xx) * 2 + cc, z if zz is None else zz)

    started = []

    def send(src, dst, name, slot, device):
        copy = pltpu.make_async_remote_copy(
            src_ref=src,
            dst_ref=dst,
            send_sem=getattr(r, name + "_s").at[slot],
            recv_sem=getattr(r, name + "_r").at[slot],
            device_id=device,
            device_id_type=MESH,
        )
        copy.start()
        started.append(copy)
        return copy

    def xp(k):
        return lax.rem(x + k, xs)

    def yp(k):
        return lax.rem(y + k, ys)

    def zp(k):
        return lax.rem(z + k, zs)

    def from_x(k):
        return lax.rem(x + xs - k, xs)

    def from_y(k):
        return lax.rem(y + ys - k, ys)

    sibling = at(cc=1 - core)
    kx, ky, kz = far_first(xs), far_first(ys), far_first(zs)

    loads = {}
    for i, name in enumerate(LOADS):
        loads[name] = pltpu.make_async_copy(hbm[name], getattr(r, name), r.load_s.at[i])
        if i < 3:
            loads[name].start()

    barrier = pltpu.get_barrier_semaphore()
    partners = [at(zz=zp(k)) for k in kz] + [at(xx=xp(k)) for k in kx] + [at(yy=yp(k)) for k in ky]
    x_pair = x + 1 - 2 * h
    partners += [sibling, at(xx=x_pair, cc=1 - core)]
    for device in partners:
        pl.semaphore_signal(barrier, inc=1, device_id=device, device_id_type=MESH)

    for name in LOADS[3:]:
        loads[name].start()
    for name in ("up", "cot", "idx"):
        loads[name].wait()
    idx = r.idx[...]
    idx16 = jnp.broadcast_to(idx, (RANK, T))

    def chosen(values):
        total = jnp.zeros((RANK, T), F32)
        for a in range(na):
            total = jnp.where(idx16 == a, values[a * RANK : (a + 1) * RANK, :], total)
        return total

    def to_blocks(values, ref):
        for b in range(8):
            kh, tb = b // 4, b % 4
            ref[b // bz, (b % bz) * 8 : (b % bz) * 8 + 8, :] = values[
                kh * 8 : kh * 8 + 8, tb * LANES : (tb + 1) * LANES
            ]

    def from_blocks(ref):
        halves = []
        for kh in range(2):
            parts = []
            for tb in range(4):
                b = kh * 4 + tb
                parts.append(ref[b // bz, (b % bz) * 8 : (b % bz) * 8 + 8, :])
            halves.append(jnp.concatenate(parts, axis=1))
        return jnp.concatenate(halves, axis=0)

    def spread_into(values, ref):
        for a in range(na):
            ref[a * RANK : (a + 1) * RANK, :] = jnp.where(idx16 == a, values, 0.0).astype(BF16)

    r.proj[...] = lax.dot_general(
        r.up[...], r.cot[...], (((0,), (0,)), ((), ())), preferred_element_type=F32
    )
    to_blocks(chosen(r.proj), r.gx)
    pl.semaphore_wait(barrier, len(partners))

    gz1 = [(k, send(r.gx.at[zp(k)], r.gr.at[k], "gz1", k, at(zz=zp(k)))) for k in kz]
    ids = lax.broadcasted_iota(jnp.int32, (LANES, T), 0)
    onehot = jnp.where(ids == jnp.broadcast_to(idx, (LANES, T)), 1.0, 0.0).astype(BF16)
    counts = lax.dot_general(
        jnp.ones((8, T), BF16), onehot, (((1,), (1,)), ((), ())), preferred_element_type=F32
    )
    r.c0[...] = counts
    cc = send(r.c0, r.c0r, "cc", 0, sibling)
    loads["down"].wait()
    loads["tok"].wait()
    r.proj[...] = lax.dot_general(
        r.down[...], r.tok[...], (((1,), (1,)), ((), ())), preferred_element_type=F32
    )
    to_blocks(chosen(r.proj), r.rx)
    rz1 = [(k, send(r.rx.at[zp(k)], r.rr.at[k], "rz1", k, at(zz=zp(k)))) for k in kz]

    total = r.gx[z]
    for k, copy in gz1:
        copy.wait_recv()
        total = total + r.gr[k]
    r.gg[z] = (0.25 * total).astype(BF16).astype(F32)
    gz2 = [(k, send(r.gg.at[z], r.gg.at[z], "gz2", k, at(zz=zp(k)))) for k in kz]

    loads["w"].wait()
    lane = lax.broadcasted_iota(jnp.int32, (T // 2, LANES), 1)
    for i in range(zs // 2):
        part = jnp.dot(
            r.tok[...], r.w[:, i * LANES : (i + 1) * LANES], preferred_element_type=F32
        )
        top, bottom = part[: T // 2], part[T // 2 :]
        r.bx[2 * i] = jnp.where(lane < Q, top, pltpu.roll(bottom, Q, 1)).astype(BF16)
        r.bx[2 * i + 1] = jnp.where(lane < Q, pltpu.roll(top, Q, 1), bottom).astype(BF16)

    total = r.rx[z]
    for k, copy in rz1:
        copy.wait_recv()
        total = total + r.rr[k]
    r.rg[z] = (SCALE * total).astype(BF16).astype(F32)
    rz2 = [(k, send(r.rg.at[z], r.rg.at[z], "rz2", k, at(zz=zp(k)))) for k in kz]

    for name in ("ma", "fa_", "sa", "mb", "fb_", "sb"):
        loads[name].wait()
    for j in range(4):
        hj, cj = j // 2, j % 2
        for i, ref in enumerate((r.ma, r.fa_, r.sa)):
            col = cj * (D // 2) + hj * LANES
            r.pfx[j, i, :, 0:LANES] = ref[:, col : col + LANES]
            r.pfx[j, i, :, LANES : 2 * LANES] = ref[:, col + 256 : col + 256 + LANES]
    for i, ref in enumerate((r.mb, r.fb_, r.sb)):
        r.pm[core, x, i] = ref[...]
    mine = r.pm.at[core, x]
    pm = [send(mine, mine, "pm", k, at(xx=xp(k))) for k in kx]
    pf = []
    for k in range(1, 4):
        hk, ck = k // 2, k % 2
        h2 = h + hk - 2 * h * hk
        c2 = core + ck - 2 * core * ck
        pf.append(
            send(
                r.pfx.at[2 * h2 + c2], r.pfr.at[q], "pf", k, at(xx=2 * m + h2, cc=c2)
            )
        )

    cc.wait_recv()
    r.c1[...] = r.c0[...] + r.c0r[...]
    cx = [(k, send(r.c1, r.c1r.at[k], "cx", k, at(xx=xp(k)))) for k in kx]

    for _, copy in gz2:
        copy.wait_recv()
    spread_into(from_blocks(r.gg), r.spread_g)
    sib = []
    for part in range(2):
        columns = pl.ds(pl.multiple_of(other_half + part * 256, 256), 256)
        r.sx[part] = jnp.dot(r.spread_g[...], r.tok[:, columns], preferred_element_type=F32)
        sib.append(send(r.sx.at[part], r.sr.at[part], "sib", part, sibling))
    for part in range(2):
        columns = pl.ds(pl.multiple_of(half + part * 256, 256), 256)
        r.own[part] = jnp.dot(r.spread_g[...], r.tok[:, columns], preferred_element_type=F32)

    total = r.c1[...]
    for k, copy in cx:
        copy.wait_recv()
        total = total + r.c1r[k]
    r.c2[...] = total
    cy = [(k, send(r.c2, r.c2r.at[k], "cy", k, at(yy=yp(k)))) for k in ky]

    def chip_sum(part, yy, xx):
        rows = pl.ds(pl.multiple_of((yy * ms + xx // 2) * RANK, RANK), RANK)
        cols = pl.ds(pl.multiple_of((xx % 2) * LANES, LANES), LANES)
        return (r.own[part, rows, cols] + r.sr[part, rows, cols]).astype(BF16)

    oy, ox = ky + [0], kx + [0]
    cuts_y = (slice(0, max(1, 3 * ys // 8)), slice(max(1, 3 * ys // 8), ys))
    cuts_x = (slice(0, max(1, 3 * xs // 8)), slice(max(1, 3 * xs // 8), xs))
    if SUM_PARTS == 1:
        cuts_y, cuts_x = (slice(0, ys),), (slice(0, xs),)
    sib[0].wait_recv()
    a1 = []
    for g, group in enumerate(cuts_y):
        for i in range(group.start, group.stop):
            for xx in range(xs):
                r.a1x[xx, i] = chip_sum(0, yp(oy[i]), xx)
        for k in kx:
            src, dst = r.a1x.at[xp(k), group], r.a1r.at[k, group]
            a1.append(send(src, dst, "a1", g * xs + k, at(xx=xp(k))))
    sib[1].wait_recv()
    b1 = []
    for g, group in enumerate(cuts_x):
        for i in range(group.start, group.stop):
            for yy in range(ys):
                r.b1x[yy, i] = chip_sum(1, yy, xp(ox[i]))
        for k in ky:
            src, dst = r.b1x.at[yp(k), group], r.b1r.at[k, group]
            b1.append(send(src, dst, "b1", g * ys + k, at(yy=yp(k))))

    for _, copy in rz2:
        copy.wait_recv()
    spread_into(from_blocks(r.rg), r.spread_r)
    cot2 = jnp.concatenate([r.cot[...], r.cot[...]], axis=0)
    grad_b = lax.dot_general(
        r.spread_r[...], cot2, (((1,), (1,)), ((), ())), preferred_element_type=F32
    )
    lane16 = lax.broadcasted_iota(jnp.int32, (RANK, LANES), 1)
    for yy in range(ys):
        for s in range(nb):
            row = (yy * ms + 2 * s) * RANK
            r.sbx[yy, s] = jnp.where(
                lane16 < Q, grad_b[row : row + RANK], grad_b[row + RANK : row + 2 * RANK]
            )
    sib.append(send(r.sbx, r.sbr, "sib", 2, sibling))

    sib[2].wait_recv()
    for yy in range(ys):
        for s in range(nb):
            r.u1x[yy, s] = (r.sbx[yy, s] + r.sbr[yy, s]).astype(BF16)
    u1 = [(k, send(r.u1x.at[yp(k)], r.u1r.at[k], "u1", k, at(yy=yp(k)))) for k in ky]

    for copy in pm:
        copy.wait_recv()
    pms = send(r.pm.at[core], r.pm.at[core], "pms", 0, sibling)

    base = [(k, send(r.bx.at[zp(k)], r.br.at[k], "bz", k, at(zz=zp(k)))) for k in kz]

    a2, b2 = [], []
    for g in range(SUM_PARTS):
        for copy in a1[g * len(kx) : (g + 1) * len(kx)]:
            copy.wait_recv()
        for i in range(cuts_y[g].start, cuts_y[g].stop):
            total = r.a1x[x, i].astype(F32)
            for k in kx:
                total = total + r.a1r[k, i].astype(F32)
            r.a2x[i] = total
            k = oy[i]
            if k:
                a2.append((k, send(r.a2x.at[i], r.a2r.at[k], "a2", k, at(yy=yp(k)))))
        for copy in b1[g * len(ky) : (g + 1) * len(ky)]:
            copy.wait_recv()
        for i in range(cuts_x[g].start, cuts_x[g].stop):
            total = r.b1x[y, i].astype(F32)
            for k in ky:
                total = total + r.b1r[k, i].astype(F32)
            r.b2x[i] = total
            k = ox[i]
            if k:
                b2.append((k, send(r.b2x.at[i], r.b2r.at[k], "b2", k, at(xx=xp(k)))))
    for _, copy in u1:
        copy.wait_recv()
    for s in range(nb):
        total = r.u1x[y, s].astype(F32)
        for k in ky:
            total = total + r.u1r[k, s].astype(F32)
        r.u2x[s] = total
    u2 = [(k, send(r.u2x, r.u2r.at[k], "u2", k, at(xx=xp(k)))) for k in kx]

    total = r.c2[...]
    for k, copy in cy:
        copy.wait_recv()
        total = total + r.c2r[k]
    lane8 = lax.broadcasted_iota(jnp.int32, (8, LANES), 1)

    def count_of(adapter):
        count = jnp.sum(jnp.where(lane8 == y * ms + adapter, total, 0.0), axis=1, keepdims=True)
        return jnp.concatenate([jnp.broadcast_to(count, (8, LANES))] * 2, axis=0)

    count16 = count_of(m)
    count_b = [jnp.where(lane16 < Q, count_of(2 * s), count_of(2 * s + 1)) for s in range(nb)]
    pms.wait_recv()

    def side_by_side(i, s):
        halves = []
        for adapter in (2 * s, 2 * s + 1):
            rows = [r.pm[j % 2, 2 * adapter + j // 2, i] for j in range(4)]
            halves.append(jnp.concatenate(rows, axis=0))
        return jnp.concatenate(halves, axis=1)

    states_b = [[side_by_side(i, s) for i in range(3)] for s in range(nb)]
    r.pfr[q] = r.pfx[q]
    for copy in pf:
        copy.wait_recv()

    def unit(i, part):
        cols = slice(part * LANES, (part + 1) * LANES)
        return jnp.concatenate([r.pfr[j, i, :, cols] for j in range(4)], axis=0)

    def update_unit(part, total):
        gradient = total * SCALE / count16
        for j in range(4):
            r.g4[j, :, part * LANES : (part + 1) * LANES] = gradient[4 * j : 4 * j + 4]
        new_master, _, _ = adam_step(unit(0, part), unit(1, part), unit(2, part), gradient)
        columns = pl.ds(pl.multiple_of(half + part * 256 + h * LANES, LANES), LANES)
        r.reta[y, m, :, columns] = new_master.astype(BF16)

    cols_a = pl.ds(pl.multiple_of(half + h * LANES, LANES), LANES)
    cols_b = pl.ds(pl.multiple_of(half + 256 + h * LANES, LANES), LANES)
    wide_b = pl.ds(pl.multiple_of(half + 256, 256), 256)

    total = r.a2x[ys - 1]
    for k, copy in a2:
        copy.wait_recv()
        total = total + r.a2r[k]
    update_unit(0, total)
    tile = r.reta.at[y, m, :, cols_a]
    ay = [(k, send(tile, tile, "ay", k, at(yy=yp(k)))) for k in ky]

    total = r.b2x[xs - 1]
    for k, copy in b2:
        copy.wait_recv()
        total = total + r.b2r[k]
    update_unit(1, total)
    tile = r.reta.at[y, m, :, cols_b]
    bx_ = [(k, send(tile, tile, "bx_", k, at(xx=xp(k)))) for k in kx]

    sums_b = [r.u2x[s] for s in range(nb)]
    for k, copy in u2:
        copy.wait_recv()
        for s in range(nb):
            sums_b[s] = sums_b[s] + r.u2r[k, s]
    for s in range(nb):
        gradient = 0.25 * sums_b[s] / count_b[s]
        r.ug[s] = gradient
        r.bt[y, s] = adam_step(*states_b[s], gradient)[0].astype(BF16)
    bby = [(k, send(r.bt.at[y], r.bt.at[y], "bby", k, at(yy=yp(k)))) for k in ky]

    odd = m % 2
    own_b = r.ug[x // 4]
    for j in range(4):
        r.bq[j] = jnp.where(odd == 1, own_b[4 * j : 4 * j + 4, Q:], own_b[4 * j : 4 * j + 4, :Q])
    new_master, new_first, new_second = adam_step(r.mb[...], r.fb_[...], r.sb[...], r.bq[q])
    r.nmb[...] = new_master
    r.nfb[...] = new_first
    r.nsb[...] = new_second

    ret = []
    for k in range(1, 4):
        hk, ck = k // 2, k % 2
        h2 = h + hk - 2 * h * hk
        c2 = core + ck - 2 * core * ck
        ret.append(
            send(r.g4.at[2 * h2 + c2], r.g4r.at[q], "ret", k, at(xx=2 * m + h2, cc=c2))
        )

    def parts_of(me, n):
        count = min(GATHER_PARTS, n // 2)
        step = 2 * (me % 2) - 1
        offsets = {4: (0, step, -step, 2), 2: (0, 1), 1: (0,)}[count]
        return count, n // count, [lax.rem(me // (n // count) + o + count, count) for o in offsets]

    def arrived(name, tile, me, source, n, device):
        slot = lax.rem(me - source + n, n)
        pltpu.make_async_remote_copy(
            src_ref=tile,
            dst_ref=tile,
            send_sem=getattr(r, name + "_s").at[slot],
            recv_sem=getattr(r, name + "_r").at[slot],
            device_id=device,
            device_id_type=MESH,
        ).wait_recv()

    early = len(started)
    column_a = r.reta.at[:, m, :, cols_a]
    row_b = r.reta.at[y, :, :, wide_b]
    tile_a, tile_b = r.reta.at[y, m, :, cols_a], r.reta.at[y, m, :, cols_b]
    ax, by = [], []
    count_y, wide_y, order_y = parts_of(y, ys)
    count_x, wide_x, order_x = parts_of(x, xs)
    for j, (pa, pb) in enumerate(zip_longest(order_y, order_x)):
        if pa is not None:
            for i in range(1 if j == 0 else 0, wide_y):
                place = lax.rem(y + i, wide_y) if j == 0 else i
                source = wide_y * pa + place
                arrived("ay", tile_a, y, source, ys, at(yy=source))
            region = r.reta.at[pl.ds(wide_y * pa, wide_y), m, :, cols_a]
            for k in kx:
                ax.append((k, send(region, region, "ax", j * xs + k, at(xx=xp(k)))))
        if pb is not None:
            for i in range(1 if j == 0 else 0, wide_x):
                place = lax.rem(x + i, wide_x) if j == 0 else i
                source = wide_x * pb + place
                arrived("bx_", tile_b, x, source, xs, at(xx=source))
            region = r.reta.at[y, pl.ds(wide_x // 2 * pb, wide_x // 2), :, wide_b]
            for k in ky:
                by.append((k, send(region, region, "by", j * ys + k, at(yy=yp(k)))))
    fa = [send(column_a, column_a, "fa", 0, sibling)]
    fb = [send(row_b, row_b, "fb", 0, sibling)]
    r.g4r[q] = r.g4[q]
    for copy in ret:
        copy.wait_recv()
    for j in range(4):
        hj, cj = j // 2, j % 2
        for part in range(2):
            col = cj * (D // 2) + part * 256 + hj * LANES
            cols = slice(col, col + LANES)
            new_master, new_first, new_second = adam_step(
                r.ma[:, cols],
                r.fa_[:, cols],
                r.sa[:, cols],
                r.g4r[j, :, part * LANES : (part + 1) * LANES],
            )
            r.nma[:, cols] = new_master
            r.nfa[:, cols] = new_first
            r.nsa[:, cols] = new_second

    term = jnp.dot(r.up[...], r.spread_r[...], preferred_element_type=F32)
    total = r.bx[z].astype(F32)
    for k, copy in base:
        copy.wait_recv()
        total = total + r.br[k].astype(F32)
    turned = jnp.transpose(total)
    r.mixed[:, : T // 2] = (turned[:Q] + 0.25 * term[:, : T // 2]).astype(BF16)
    r.mixed[:, T // 2 :] = (turned[Q:] + 0.25 * term[:, T // 2 :]).astype(BF16)

    for copy in started[:early]:
        copy.wait_send()

    for k in kx:
        for other, copy in ax:
            if other == k:
                copy.wait_recv()
        source = from_x(k)
        region = r.reta.at[
            :,
            source // 2,
            :,
            pl.ds(pl.multiple_of(half + (source % 2) * LANES, LANES), LANES),
        ]
        fa.append(send(region, region, "fa", k, sibling))
    for k in ky:
        for other, copy in by:
            if other == k:
                copy.wait_recv()
        region = r.reta.at[from_y(k), :, :, wide_b]
        fb.append(send(region, region, "fb", k, sibling))
    for _, copy in bby:
        copy.wait_recv()
    for yy in range(ys):
        for s in range(nb):
            both = r.bt[yy, s].astype(F32)
            row = (yy * ms + 2 * s) * RANK
            r.ball[row : row + RANK, :] = both
            r.ball[row + RANK : row + 2 * RANK, :] = pltpu.roll(both, Q, 1)
    r.retb[...] = jnp.transpose(r.ball[...])[:Q].astype(BF16)
    for copy in fa + fb:
        copy.wait_recv()
    for copy in started[early:]:
        copy.wait_send()


def place(*refs):
    sems = refs[18]
    copies = [pltpu.make_async_copy(refs[i], refs[9 + i], sems.at[i]) for i in range(9)]
    for copy in copies:
        copy.start()
    for copy in copies:
        copy.wait()


def shards(ys, xs, zs, tok, w, down, up, cot, idx, ma, mb, fa, sa, fb, sb):
    ms = xs // 2
    c_rows = ys * ms * RANK
    order, shapes = scratch(ys, xs, zs)
    vmem = pl.BlockSpec(memory_space=pltpu.VMEM)
    hbm = pl.BlockSpec(memory_space=pl.ANY)
    own, own_b = ((4, D), F32), ((4, Q), F32)
    results = (
        ((Q, T), BF16), own, own_b, own, own, own_b, own_b,
        ((ys, ms, RANK, D), BF16), ((Q, c_rows), BF16),
    )
    out = pl.pallas_call(
        functools.partial(kernel, ys, xs, zs, order),
        out_shape=tuple(pltpu.VMEM(shape, dtype) for shape, dtype in results),
        in_specs=[hbm] * 12,
        out_specs=(vmem,) * 9,
        scratch_shapes=shapes,
        compiler_params=pltpu.CompilerParams(
            collective_id=0, has_side_effects=True, vmem_limit_bytes=56 * 1024 * 1024
        ),
    )(tok, w, down, up.T, cot.T, idx.T, ma, mb, fa, sa, fb, sb)
    out = pl.pallas_call(
        place,
        out_shape=tuple(jax.ShapeDtypeStruct(shape, dtype) for shape, dtype in results),
        in_specs=[vmem] * 9,
        out_specs=(hbm,) * 9,
        scratch_shapes=[pltpu.SemaphoreType.DMA((9,))],
    )(*(pltpu.with_memory_space_constraint(o, pltpu.VMEM) for o in out))
    mixed, nma, nmb, nfa, nsa, nfb, nsb, reta, retb = out
    return (mixed.T, nma, nmb, nfa, nsa, nfb, nsb, reta.reshape(c_rows, D), retb.T)


def build(mesh, ys, xs, zs):
    both, width = P("dp", "fsdp"), P(None, "fsdp")
    return jax.shard_map(
        functools.partial(shards, ys, xs, zs),
        mesh=mesh,
        in_specs=(both, P("fsdp", None), width, width, both, P("dp", None)) + (both,) * 6,
        out_specs=(both,) * 7 + (width, width),
        check_vma=False,
    )


def solution(mesh):
    return build(mesh, YS, XS, ZS)
```
